32 devices in a mesh: seq: 8 (over y, x, core), head: 4 (over z).
Axes of the slice: x: 2, y: 2, z: 4, core: 2. Of those that a mesh axis runs over, the one named last changes fastest.
Arguments:
- queries: bfloat16 [2048, 5120], P(('seq', 'head')), may hold values from -12 to 12
- keys: bfloat16 [2048, 5120], P(('seq', 'head')), may hold values from -12 to 12
- values: bfloat16 [2048, 5120], P(('seq', 'head')), may hold values from -6 to 6
- out_grad: bfloat16 [2048, 5120], P(('seq', 'head')), may hold values from -6 to 6
- chain_lengths: int32 [16], replicated, may hold values from 1 to 512, 2048 in all
- block_pairs: int32 [16, 4], replicated, may hold values from -1 to 15, as said below
Outputs:
- attn_out: bfloat16 [2048, 5120], P(('seq', 'head'))
- query_grad: bfloat16 [2048, 5120], P(('seq', 'head'))
- key_grad: bfloat16 [2048, 5120], P(('seq', 'head'))
- value_grad: bfloat16 [2048, 5120], P(('seq', 'head'))
The draws below stay inside these ranges and needn't reach their ends.
Inputs may be any that keep to these rules, and one draw needn't show every extreme that they name: `block_pairs`: row q lists the key blocks that query block q attends to. Slot 0 holds q itself; the other live entries are distinct blocks of the same or an adjacent sequence shard of 256 tokens, in no particular order; empty slots hold -1 and follow the live ones. Every row has 2 or more live entries, and in every draw some row has 4.
All inputs are finite; a program needn't handle non-finite values.
Results may differ from the reference program's by a relative error of at most 0.023.
Values may be sent and summed in bfloat16 or wider, within the bound.
No kernel may reach another device: no remote copies, remote signals or barrier semaphores. Data moves between devices by JAX's collectives and lax.ppermute only.
A program may use at most 128 MiB of HBM per device.

```python
import math
import jax
import jax.numpy as jnp
import numpy as np
from jax import lax

D = 5120
HEADS = 40
HEAD_SIZE = 128
TOK_DEV = 256
BLOCK_TOKENS = 128
PAIRS = 4
TOKENS = 2048
CHAINS = 16
CHAIN_MOST = 512


def paired_heads(key):
    base = jax.random.fold_in(key, 7)
    streams = jax.random.split(base, 4)
    query_draw = jnp.clip(jax.random.normal(streams[2], (TOKENS, D)), -6.0, 6.0)
    key_draw = jnp.clip(jax.random.normal(streams[3], (TOKENS, D)), -6.0, 6.0)
    return (query_draw, key_draw)


def draw_queries(key, part):
    return paired_heads(key)[0].astype(jnp.bfloat16)


def draw_keys(key, part):
    return paired_heads(key)[1].astype(jnp.bfloat16)


def draw_block_pairs(key, part):
    nshards = TOKENS // TOK_DEV
    per_shard = TOK_DEV // BLOCK_TOKENS
    nblocks = TOKENS // BLOCK_TOKENS
    width = 3 * per_shard
    base = jax.random.fold_in(key, 11)
    streams = jax.random.split(base, 5)
    block_index = jnp.arange(nblocks, dtype=jnp.int32)
    shard_of = block_index // per_shard
    candidate = (shard_of[:, None] - 1) * per_shard + jnp.arange(width, dtype=jnp.int32)[None, :]
    usable = (candidate >= 0) & (candidate < nblocks) & (candidate != block_index[:, None])
    ranking = jax.random.randint(streams[0], (nblocks, width), 0, 1 << 20) * width + jnp.arange(width, dtype=jnp.int32)[None, :]
    ranking = jnp.where(usable, ranking, 1 << 30)
    order = jnp.argsort(ranking, axis=1, stable=True)
    picked = jnp.take_along_axis(candidate, order, axis=1)[:, :PAIRS - 1]
    shard_top = jax.random.randint(streams[1], (nshards,), 3, PAIRS + 1)
    busiest = jax.random.randint(streams[2], (), 0, nshards)
    shard_top = jnp.where(jnp.arange(nshards) == busiest, PAIRS, shard_top)
    row_top = shard_top[shard_of]
    spread = jax.random.randint(streams[3], (nblocks,), 0, 1 << 20)
    counts = 2 + spread % (row_top - 1)
    full_row = jax.random.randint(streams[4], (nshards,), 0, per_shard)
    counts = jnp.where(block_index % per_shard == full_row[shard_of], row_top, counts)
    slot_number = jnp.arange(PAIRS - 1, dtype=jnp.int32)
    others = jnp.where(slot_number[None, :] < (counts - 1)[:, None], picked, -1)
    return jnp.concatenate([block_index[:, None], others], axis=1).astype(jnp.int32)


def levels(rng, dims, cuts, low, top_value):
    gain, own = 1.0, jax.random.fold_in(rng, 6)
    for dim, blocks in cuts:
        draws = jnp.exp(jax.random.uniform(jax.random.fold_in(own, dim), (blocks,), jnp.float32, low / len(cuts), top_value / len(cuts)))
        gain = gain * jnp.repeat(draws, dims[dim] // blocks).reshape([-1 if axis == dim else 1 for axis in range(len(dims))])
    return gain


def profile(number_of, total, bound, lean):
    loads = [(1 << 20) // math.isqrt(standing ** lean) + 1 for standing in range(2, number_of + 1)]
    rest, holding = total - bound - (number_of - 1), [1] * (number_of - 1)
    while rest > 0:
        free = [i for i in range(number_of - 1) if holding[i] < bound]
        pool, budget = sum([loads[i] for i in free]), rest
        for i in free:
            addition = min(bound - holding[i], max(1, budget * loads[i] // pool), rest)
            holding[i] = holding[i] + addition
            rest = rest - addition
    return np.array([bound] + holding)


def uneven(key, count, total, limit, skew):
    if count == 2:
        one = jax.random.randint(key, (), max(1, total - limit), min(limit, total - 1) + 1)
        return jnp.stack([one, total - one])
    tallies = jnp.asarray(profile(count, total, limit, skew), jnp.int32)
    pairs = (count - 1) // 2
    donor, receiver = tallies[1:1 + 2 * pairs:2], tallies[2:2 + 2 * pairs:2]
    margin = jnp.minimum(donor - 1, limit - receiver)
    moved = jax.random.randint(jax.random.fold_in(key, 1), (pairs,), 0, 1 << 20) % (margin + 1)
    tallies = tallies.at[1:1 + 2 * pairs:2].set(donor - moved).at[2:2 + 2 * pairs:2].set(receiver + moved)
    return tallies[jax.random.permutation(jax.random.fold_in(key, 2), count)]


def gaussian(stream_key, dims, scale, limit, cuts=(), held_as=jnp.bfloat16):
    factor_of = levels(stream_key, dims, cuts, -0.22, 0.18) if cuts else 1.0
    values = jax.random.normal(stream_key, dims, jnp.float32) * scale * factor_of
    return jnp.minimum(jnp.maximum(values, -limit), limit).astype(held_as)


def setup_inputs(seed: int = 0) -> dict:
    seeds = jax.random.split(jax.random.key(seed), 7)
    queries = draw_queries(jax.random.fold_in(seeds[6], 71), 0)
    keys = draw_keys(jax.random.fold_in(seeds[6], 71), 0)
    values = gaussian(seeds[2], (TOKENS, D), 1.0, 6.0, ((0, 32),))
    out_grad = gaussian(seeds[3], (TOKENS, D), 1.0, 6.0, ((0, 32),))
    chain_lengths = uneven(seeds[4], CHAINS, TOKENS, CHAIN_MOST, 2).astype(jnp.int32)
    block_pairs = draw_block_pairs(jax.random.fold_in(seeds[6], 71), 0)
    return {"queries": queries, "keys": keys, "values": values, "out_grad": out_grad, "chain_lengths": chain_lengths, "block_pairs": block_pairs}


masked_score = -1e+30
rotary_base = 10000.0

def rotary_tables(position, half_width):
    column_index = jnp.arange(half_width).astype(jnp.float32)
    frequency = jnp.exp(column_index * (-2.0 * math.log(rotary_base) / (2 * half_width)))
    angle = position.astype(jnp.float32)[:, None] * frequency[None, :]
    return (jnp.cos(angle)[:, None, :], jnp.sin(angle)[:, None, :])

def rotate(values_in, cosine, sine_table):
    half_width = values_in.shape[-1] // 2
    first_half = values_in[..., :half_width]
    second_half = values_in[..., half_width:]
    return jnp.concatenate([first_half * cosine - second_half * sine_table, second_half * cosine + first_half * sine_table], axis=-1)

def unrotate(grads_in, cosine, sine_table):
    half_width = grads_in.shape[-1] // 2
    first_half = grads_in[..., :half_width]
    second_half = grads_in[..., half_width:]
    return jnp.concatenate([first_half * cosine + second_half * sine_table, second_half * cosine - first_half * sine_table], axis=-1)

def chain_positions(chain_lengths, token_rows):
    lengths32 = chain_lengths.astype(jnp.int32)
    starts = (jnp.cumsum(lengths32) - lengths32).astype(jnp.int32)
    begins = lax.optimization_barrier(jnp.max(jnp.where(starts[None, :] <= token_rows[:, None], starts[None, :], 0), axis=1))
    return (token_rows - begins).astype(jnp.int32)

def reference(queries, keys, values, out_grad, chain_lengths, block_pairs):
    total = queries.shape[0]
    nblocks = total // BLOCK_TOKENS
    score_scale = 1.0 / math.sqrt(HEAD_SIZE)
    position = chain_positions(chain_lengths, jnp.arange(total, dtype=jnp.int32))
    cosine, sine_table = rotary_tables(position, HEAD_SIZE // 2)
    head_shape = (total, HEADS, HEAD_SIZE)
    query_rot = rotate(queries.reshape(head_shape).astype(jnp.float32), cosine, sine_table).astype(jnp.bfloat16)
    key_rot = rotate(keys.reshape(head_shape).astype(jnp.float32), cosine, sine_table).astype(jnp.bfloat16)
    value_heads = values.reshape(head_shape)
    grad_heads = out_grad.reshape(head_shape)
    key_block_rows = key_rot.reshape(nblocks, BLOCK_TOKENS, HEADS, HEAD_SIZE)
    value_blocks = value_heads.reshape(nblocks, BLOCK_TOKENS, HEADS, HEAD_SIZE)

    def step(carry, block_index):
        key_acc, value_acc = carry
        listed = block_pairs[block_index]
        live_slot = listed >= 0
        safe_slot = jnp.where(live_slot, listed, 0).astype(jnp.int32)
        query_block = lax.dynamic_slice_in_dim(query_rot, block_index * BLOCK_TOKENS, BLOCK_TOKENS, 0).astype(jnp.float32)
        grad_block = lax.dynamic_slice_in_dim(grad_heads, block_index * BLOCK_TOKENS, BLOCK_TOKENS, 0).astype(jnp.float32)
        key_rows = key_block_rows[safe_slot].astype(jnp.float32)
        value_rows = value_blocks[safe_slot].astype(jnp.float32)
        score = jnp.einsum('qhd,pkhd->hqpk', query_block, key_rows) * score_scale
        score = jnp.where(live_slot[None, None, :, None], score, masked_score)
        row_top = lax.optimization_barrier(jnp.max(score, axis=(2, 3), keepdims=True))
        log_total = row_top + jnp.log(lax.optimization_barrier(jnp.sum(jnp.exp(score - row_top), axis=(2, 3), keepdims=True)))
        probability = jnp.exp(score - log_total)
        weights = probability.astype(jnp.bfloat16)
        attention = jnp.einsum('hqpk,pkhd->qhd', weights.astype(jnp.float32), value_rows).astype(jnp.bfloat16)
        row_delta = lax.optimization_barrier(jnp.sum(grad_block * attention.astype(jnp.float32), axis=-1))
        grad_prob = jnp.einsum('qhd,pkhd->hqpk', grad_block, value_rows)
        grad_score = (probability * (grad_prob - row_delta.T[:, :, None, None]) * score_scale).astype(jnp.bfloat16)
        grad_score32 = grad_score.astype(jnp.float32)
        query_grad_rot = jnp.einsum('hqpk,pkhd->qhd', grad_score32, key_rows)
        key_terms = jnp.einsum('hqpk,qhd->pkhd', grad_score32, query_block)
        value_terms = jnp.einsum('hqpk,qhd->pkhd', weights.astype(jnp.float32), grad_block)
        live_weight = live_slot.astype(jnp.float32)[:, None, None, None]
        key_acc = key_acc.at[safe_slot].add(key_terms * live_weight)
        value_acc = value_acc.at[safe_slot].add(value_terms * live_weight)
        return ((key_acc, value_acc), (attention, query_grad_rot))
    empty = jnp.zeros((nblocks, BLOCK_TOKENS, HEADS, HEAD_SIZE), jnp.float32)
    (key_acc, value_acc), (attn_blocks, query_blocks) = lax.scan(step, (empty, empty), jnp.arange(nblocks, dtype=jnp.int32))
    attn_out = attn_blocks.reshape(total, HEADS * HEAD_SIZE)
    query_grad = unrotate(query_blocks.reshape(head_shape), cosine, sine_table).astype(jnp.bfloat16).reshape(total, HEADS * HEAD_SIZE)
    key_grad = unrotate(key_acc.reshape(head_shape), cosine, sine_table).astype(jnp.bfloat16).reshape(total, HEADS * HEAD_SIZE)
    value_grad = value_acc.reshape(total, HEADS * HEAD_SIZE).astype(jnp.bfloat16)
    return (attn_out, query_grad, key_grad, value_grad)
```

```python
import functools
import math

import jax
import jax.numpy as jnp
from jax import lax
from jax.experimental import pallas as pl
from jax.experimental.pallas import tpu as pltpu
from jax.sharding import PartitionSpec as P

HEAD_SIZE = 128
BLOCK_TOKENS = 128
HALF = HEAD_SIZE // 2
SCALE = 1.0 / math.sqrt(HEAD_SIZE)
VMEM_LIMIT = 48 * 1024 * 1024

masked_score = -1e30
rotary_base = 10000.0

SMEM_SPEC = pl.BlockSpec(memory_space=pltpu.SMEM)
VMEM_SPEC = pl.BlockSpec(memory_space=pltpu.VMEM)


def cost(flops, moved, exps=0):
    return pl.CostEstimate(flops=flops, bytes_accessed=moved, transcendentals=exps)


def params():
    return pltpu.CompilerParams(vmem_limit_bytes=VMEM_LIMIT)


def rotary_tables(position):
    column_index = jnp.arange(HALF).astype(jnp.float32)
    frequency = jnp.exp(column_index * (-2.0 * math.log(rotary_base) / HEAD_SIZE))
    angle = position.astype(jnp.float32)[:, None] * frequency[None, :]
    cosine, sine = jnp.cos(angle), jnp.sin(angle)
    return (
        jnp.concatenate([cosine, cosine], axis=1),
        jnp.concatenate([-sine, sine], axis=1),
    )


def chain_positions(chain_lengths, token_rows):
    starts = jnp.cumsum(chain_lengths) - chain_lengths
    begins = jnp.max(jnp.where(starts[None, :] <= token_rows[:, None], starts[None, :], 0), axis=1)
    return token_rows - begins


def rotate(x, cosine, sine):
    return x * cosine + pltpu.roll(x, HALF, 1) * sine


def unrotate(g, cosine, sine):
    return g * cosine - pltpu.roll(g, HALF, 1) * sine


def piece_rows(meta, step, rows):
    return pl.ds(pl.multiple_of(jnp.bitwise_xor(meta[0], step) * rows, rows), rows)


def dot(a, b, contract):
    return lax.dot_general(a, b, (contract, ((), ())), preferred_element_type=jnp.float32)


def cut_kernel(turned, meta, cosine, sine, *refs):
    count = len(turned)
    sources, pieces = refs[:count], refs[count:]
    width = pieces[0].shape[-1]
    for step, piece in enumerate(pieces):
        base = jnp.bitwise_xor(meta[0], step) * width
        for t in range(count):
            for h in range(0, width, HEAD_SIZE):
                x = sources[t][:, pl.ds(pl.multiple_of(base + h, HEAD_SIZE), HEAD_SIZE)]
                if turned[t]:
                    x = rotate(x.astype(jnp.float32), cosine[...], sine[...]).astype(x.dtype)
                piece[t, :, h : h + HEAD_SIZE] = x


def cut(turned, meta, cosine, sine, arrays, n):
    rows, width = arrays[0].shape
    shape = jax.ShapeDtypeStruct((len(arrays), rows, width // n), arrays[0].dtype)
    return pl.pallas_call(
        functools.partial(cut_kernel, turned),
        out_shape=[shape] * n,
        in_specs=[SMEM_SPEC] + [VMEM_SPEC] * (2 + len(arrays)),
        out_specs=[VMEM_SPEC] * n,
        compiler_params=params(),
        cost_estimate=cost(0, 4 * len(arrays) * rows * width),
        name="cut",
    )(meta, cosine, sine, *arrays)


def order_kernel(meta, *refs):
    pieces, out = refs[:-1], refs[-1]
    rows = pieces[0].shape[1]
    for step, piece in enumerate(pieces):
        out[:, piece_rows(meta, step, rows), :] = piece[...]


def order(meta, pieces):
    count, rows, width = pieces[0].shape
    n = len(pieces)
    return pl.pallas_call(
        order_kernel,
        out_shape=jax.ShapeDtypeStruct((count, n * rows, width), pieces[0].dtype),
        in_specs=[SMEM_SPEC] + [VMEM_SPEC] * n,
        out_specs=VMEM_SPEC,
        compiler_params=params(),
        cost_estimate=cost(0, 4 * n * count * rows * width),
        name="order",
    )(meta, *pieces)


def join_kernel(count, meta, *refs):
    pieces, outs = refs[:-count], refs[-count:]
    width = pieces[0].shape[-1]
    for step, piece in enumerate(pieces):
        base = pl.multiple_of(jnp.bitwise_xor(meta[0], step) * width, HEAD_SIZE)
        for t, out in enumerate(outs):
            out[:, pl.ds(base, width)] = piece[t]


def join(meta, pieces):
    count, rows, width = pieces[0].shape
    n = len(pieces)
    return pl.pallas_call(
        functools.partial(join_kernel, count),
        out_shape=[jax.ShapeDtypeStruct((rows, n * width), pieces[0].dtype)] * count,
        in_specs=[SMEM_SPEC] + [VMEM_SPEC] * n,
        out_specs=[VMEM_SPEC] * count,
        compiler_params=params(),
        cost_estimate=cost(0, 4 * n * count * rows * width),
        name="join",
    )(meta, *pieces)


def window_rows(win, meta, which, block, pairs, lanes):
    return jnp.concatenate(
        [
            win[which, pl.ds(pl.multiple_of(meta[1 + block * pairs + p] * BLOCK_TOKENS, BLOCK_TOKENS), BLOCK_TOKENS), lanes]
            for p in range(pairs)
        ],
        axis=0,
    )


def scores(query, key_rows, meta, block, nblk, pairs):
    score = dot(query, key_rows, ((1,), (1,))) * SCALE
    parts = []
    for p in range(pairs):
        part = score[:, p * BLOCK_TOKENS : (p + 1) * BLOCK_TOKENS]
        live = meta[1 + nblk * pairs + block * pairs + p] > 0
        parts.append(jnp.where(live, part, masked_score))
    return jnp.concatenate(parts, axis=1)


def fill_window(win, low, mid, high):
    length = mid.shape[1]
    for i, part in enumerate((low, mid, high)):
        win[:, i * length : (i + 1) * length, :] = part[...]


def forward_kernel(n, nblk, pairs, meta, low, mid, high, *refs):
    query_pieces, out_pieces = refs[:n], refs[n : 2 * n]
    lse_ref, win, query_s, out_s = refs[2 * n :]
    rows = query_pieces[0].shape[1]
    fill_window(win, low, mid, high)
    for step, piece in enumerate(query_pieces):
        query_s[piece_rows(meta, step, rows), :] = piece[0]
    for block in range(nblk):
        here = slice(block * BLOCK_TOKENS, (block + 1) * BLOCK_TOKENS)
        for h in range(query_s.shape[1] // HEAD_SIZE):
            lanes = slice(h * HEAD_SIZE, (h + 1) * HEAD_SIZE)
            key_rows = window_rows(win, meta, 0, block, pairs, lanes)
            value_rows = window_rows(win, meta, 1, block, pairs, lanes)
            score = scores(query_s[here, lanes], key_rows, meta, block, nblk, pairs)
            top = jnp.max(score, axis=1, keepdims=True)
            raised = jnp.exp(score - top)
            total = jnp.sum(raised, axis=1, keepdims=True)
            weights = (raised / total).astype(jnp.bfloat16)
            out_s[here, lanes] = dot(weights, value_rows, ((1,), (0,))).astype(jnp.bfloat16)
            lse_ref[here, lanes] = jnp.broadcast_to(top + jnp.log(total), (BLOCK_TOKENS, HEAD_SIZE))
    for step, piece in enumerate(out_pieces):
        piece[0] = out_s[piece_rows(meta, step, rows), :]


def backward_kernel(n, nblk, pairs, meta, cosine, sine, low, mid, high, lse_ref, *refs):
    inputs, out_pieces, grad_pieces = refs[:n], refs[n : 2 * n], refs[2 * n : 3 * n]
    lower, upper, own, win, query_s, grad_s, out_s, key_acc, value_acc = refs[3 * n :]
    rows = inputs[0].shape[1]
    length = mid.shape[1]
    fill_window(win, low, mid, high)
    for step in range(n):
        place = piece_rows(meta, step, rows)
        query_s[place, :] = inputs[step][0]
        grad_s[place, :] = inputs[step][1]
        out_s[place, :] = out_pieces[step][0]
    key_acc[...] = jnp.zeros_like(key_acc)
    value_acc[...] = jnp.zeros_like(value_acc)
    for block in range(nblk):
        here = slice(block * BLOCK_TOKENS, (block + 1) * BLOCK_TOKENS)
        for h in range(query_s.shape[1] // HEAD_SIZE):
            lanes = slice(h * HEAD_SIZE, (h + 1) * HEAD_SIZE)
            key_rows = window_rows(win, meta, 0, block, pairs, lanes)
            value_rows = window_rows(win, meta, 1, block, pairs, lanes)
            query, grad = query_s[here, lanes], grad_s[here, lanes]
            score = scores(query, key_rows, meta, block, nblk, pairs)
            log_total = jnp.concatenate([lse_ref[here, lanes]] * pairs, axis=1)
            probability = jnp.exp(score - log_total)
            weights = probability.astype(jnp.bfloat16)
            delta = jnp.sum(
                grad.astype(jnp.float32) * out_s[here, lanes].astype(jnp.float32), axis=1, keepdims=True
            )
            grad_prob = dot(grad, value_rows, ((1,), (1,)))
            grad_score = (probability * (grad_prob - delta) * SCALE).astype(jnp.bfloat16)
            query_grad = dot(grad_score, key_rows, ((1,), (0,)))
            out_s[here, lanes] = unrotate(query_grad, cosine[here, :], sine[here, :]).astype(jnp.bfloat16)
            key_terms = dot(grad_score, query, ((0,), (0,)))
            value_terms = dot(weights, grad, ((0,), (0,)))
            for p in range(pairs):
                slot = pl.ds(
                    pl.multiple_of(meta[1 + block * pairs + p] * BLOCK_TOKENS, BLOCK_TOKENS), BLOCK_TOKENS
                )
                part = slice(p * BLOCK_TOKENS, (p + 1) * BLOCK_TOKENS)
                key_acc[slot, lanes] += key_terms[part]
                value_acc[slot, lanes] += value_terms[part]
    for step, piece in enumerate(grad_pieces):
        piece[0] = out_s[piece_rows(meta, step, rows), :]
    for t, acc in enumerate((key_acc, value_acc)):
        lower[t] = acc[:length, :].astype(jnp.bfloat16)
        own[t] = acc[length : 2 * length, :]
        upper[t] = acc[2 * length :, :].astype(jnp.bfloat16)


def columns(shape, lanes):
    lead = (0,) * (len(shape) - 1)
    return pl.BlockSpec(tuple(shape[:-1]) + (lanes,), lambda i: lead + (i,))


def forward(meta, nblk, pairs, low, mid, high, query_pieces, lanes):
    n = len(query_pieces)
    _, length, width = mid.shape
    rows = length // n
    window = columns(mid.shape, lanes)
    piece = columns((1, rows, width), lanes)
    out = jax.ShapeDtypeStruct((1, rows, width), jnp.bfloat16)
    results = pl.pallas_call(
        functools.partial(forward_kernel, n, nblk, pairs),
        grid=(width // lanes,),
        out_shape=[out] * n + [jax.ShapeDtypeStruct((length, width), jnp.float32)],
        in_specs=[SMEM_SPEC] + [window] * 3 + [piece] * n,
        out_specs=[piece] * n + [columns((length, width), lanes)],
        scratch_shapes=[
            pltpu.VMEM((2, 3 * length, lanes), jnp.bfloat16),
            pltpu.VMEM((length, lanes), jnp.bfloat16),
            pltpu.VMEM((length, lanes), jnp.bfloat16),
        ],
        compiler_params=params(),
        cost_estimate=cost(4 * length * pairs * BLOCK_TOKENS * width, 20 * length * width),
        name="forward",
    )(meta, low, mid, high, *query_pieces)
    return results[:n], results[n]


def backward(meta, nblk, pairs, cosine, sine, low, mid, high, lse, inputs, out_pieces, lanes):
    n = len(inputs)
    _, length, width = mid.shape
    rows = length // n
    window = columns(mid.shape, lanes)
    piece = columns((1, rows, width), lanes)
    pair_piece = columns((2, rows, width), lanes)
    table = pl.BlockSpec(cosine.shape, lambda i: (0, 0))
    out = jax.ShapeDtypeStruct((1, rows, width), jnp.bfloat16)
    results = pl.pallas_call(
        functools.partial(backward_kernel, n, nblk, pairs),
        grid=(width // lanes,),
        out_shape=[out] * n
        + [jax.ShapeDtypeStruct(mid.shape, jnp.bfloat16)] * 2
        + [jax.ShapeDtypeStruct(mid.shape, jnp.float32)],
        in_specs=[SMEM_SPEC, table, table]
        + [window] * 3
        + [columns((length, width), lanes)]
        + [pair_piece] * n
        + [piece] * n,
        out_specs=[piece] * n + [window] * 3,
        scratch_shapes=[
            pltpu.VMEM((2, 3 * length, lanes), jnp.bfloat16),
            pltpu.VMEM((length, lanes), jnp.bfloat16),
            pltpu.VMEM((length, lanes), jnp.bfloat16),
            pltpu.VMEM((length, lanes), jnp.bfloat16),
            pltpu.VMEM((3 * length, lanes), jnp.float32),
            pltpu.VMEM((3 * length, lanes), jnp.float32),
        ],
        compiler_params=params(),
        cost_estimate=cost(10 * length * pairs * BLOCK_TOKENS * width, 40 * length * width),
        name="backward",
    )(meta, cosine, sine, low, mid, high, lse, *inputs, *out_pieces)
    return results[:n], results[n], results[n + 1], results[n + 2]


def combine_kernel(meta, cosine, sine, own, from_upper, from_lower, *pieces):
    rows = pieces[0].shape[1]
    for step, piece in enumerate(pieces):
        place = piece_rows(meta, step, rows)
        for h in range(0, own.shape[2], HEAD_SIZE):
            lanes = slice(h, h + HEAD_SIZE)
            for t in range(2):
                total = (
                    own[t, place, lanes]
                    + from_upper[t, place, lanes].astype(jnp.float32)
                    + from_lower[t, place, lanes].astype(jnp.float32)
                )
                if t == 0:
                    total = unrotate(total, cosine[place, :], sine[place, :])
                piece[t, :, lanes] = total.astype(jnp.bfloat16)


def combine(meta, cosine, sine, own, from_upper, from_lower, n):
    count, length, width = own.shape
    shape = jax.ShapeDtypeStruct((count, length // n, width), jnp.bfloat16)
    return pl.pallas_call(
        combine_kernel,
        out_shape=[shape] * n,
        in_specs=[SMEM_SPEC] + [VMEM_SPEC] * 5,
        out_specs=[VMEM_SPEC] * n,
        compiler_params=params(),
        cost_estimate=cost(0, 10 * count * length * width),
        name="combine",
    )(meta, cosine, sine, own, from_upper, from_lower)


def swap(pieces):
    n = len(pieces)
    return [pieces[0]] + [
        lax.ppermute(pieces[k], "head", [(i, i ^ k) for i in range(n)]) for k in range(1, n)
    ]


def shift(block, distance):
    devices = range(lax.axis_size("seq"))
    return lax.ppermute(block, "seq", [(i, i + distance) for i in devices if i + distance in devices])


def on_device(queries, keys, values, out_grad, chain_lengths, block_pairs):
    n = lax.axis_size("head")
    me = lax.axis_index("head")
    shard = lax.axis_index("seq")
    rows = queries.shape[0]
    length = rows * n
    nblk = length // BLOCK_TOKENS
    pairs = block_pairs.shape[1]

    token_rows = shard * length + jnp.arange(length, dtype=jnp.int32)
    own_rows = shard * length + me * rows + jnp.arange(rows, dtype=jnp.int32)
    own_cos, own_sin = rotary_tables(chain_positions(chain_lengths, own_rows))
    cosine, sine = rotary_tables(chain_positions(chain_lengths, token_rows))
    ids = lax.dynamic_slice_in_dim(block_pairs, shard * nblk, nblk, 0)
    live = ids >= 0
    slots = jnp.where(live, ids - (shard - 1) * nblk, 0)
    meta = jnp.concatenate(
        [me.reshape(1), slots.reshape(-1), live.astype(jnp.int32).reshape(-1)]
    ).astype(jnp.int32)

    key_value = swap(cut((True, False), meta, own_cos, own_sin, (keys, values), n))
    inputs = swap(cut((True, False), meta, own_cos, own_sin, (queries, out_grad), n))
    mid = order(meta, key_value)
    low, high = shift(mid, 1), shift(mid, -1)
    lanes = 2 * HEAD_SIZE
    out_pieces, lse = forward(meta, nblk, pairs, low, mid, high, inputs, lanes)
    back_out = swap(out_pieces)
    grad_pieces, lower, upper, own = backward(
        meta, nblk, pairs, cosine, sine, low, mid, high, lse, inputs, out_pieces, lanes
    )
    back_grad = swap(grad_pieces)
    from_upper, from_lower = shift(lower, -1), shift(upper, 1)
    back_kv = swap(combine(meta, cosine, sine, own, from_upper, from_lower, n))
    (attn_out,) = join(meta, back_out)
    (query_grad,) = join(meta, back_grad)
    key_grad, value_grad = join(meta, back_kv)
    return attn_out, query_grad, key_grad, value_grad


def solution(mesh):
    split = P(("seq", "head"), None)
    return jax.shard_map(
        on_device,
        mesh=mesh,
        in_specs=(split, split, split, split, P(), P()),
        out_specs=(split, split, split, split),
        check_vma=False,
    )
```

```python
import functools
import math

import jax
import jax.numpy as jnp
from jax import lax
from jax.experimental import pallas as pl
from jax.experimental.pallas import tpu as pltpu
from jax.sharding import PartitionSpec as P

HEAD_SIZE = 128
BLOCK_TOKENS = 128
HALF = HEAD_SIZE // 2
SCALE = 1.0 / math.sqrt(HEAD_SIZE)
VMEM_LIMIT = 32 * 1024 * 1024
WIDE_LIMIT = 60 * 1024 * 1024

masked_score = -1e30
rotary_base = 10000.0

SMEM_SPEC = pl.BlockSpec(memory_space=pltpu.SMEM)


def cost(flops, moved, exps=0):
    return pl.CostEstimate(flops=flops, bytes_accessed=moved, transcendentals=exps)


def params(limit=VMEM_LIMIT):
    return pltpu.CompilerParams(vmem_limit_bytes=limit)


def behind(kernel, count):
    def run(*refs):
        kernel(*refs[count:])

    return run if count else kernel


ANY_SPEC = pl.BlockSpec(memory_space=pl.ANY)
HBM_SPEC = pl.BlockSpec(memory_space=pltpu.HBM)
VMEM_SPEC = pl.BlockSpec(memory_space=pltpu.VMEM)


def chain_angles(lengths, first_row, shape, tokens):
    row = first_row + lax.broadcasted_iota(jnp.int32, shape, tokens)

    def look(c, carry):
        start, begin = carry
        return start + lengths[c], jnp.maximum(begin, jnp.where(row >= start, start, 0))

    _, begin = lax.fori_loop(
        0, lengths.shape[0], look, (jnp.int32(0), jnp.zeros(shape, jnp.int32))
    )
    entry = lax.broadcasted_iota(jnp.int32, shape, 1 - tokens)
    column = jnp.where(entry < HALF, entry, entry - HALF).astype(jnp.float32)
    frequency = jnp.exp(column * (-2.0 * math.log(rotary_base) / HEAD_SIZE))
    return (row - begin).astype(jnp.float32) * frequency, entry


def fill_tables(lengths, first_row, cosine, sine, scale=1.0):
    angle, entry = chain_angles(lengths, first_row, cosine.shape, 0)
    turn = jnp.sin(angle) * scale
    cosine[...] = jnp.cos(angle) * scale
    sine[...] = jnp.where(entry < HALF, -turn, turn)


def rotate(x, cosine, sine):
    return x * cosine + pltpu.roll(x, HALF, 1) * sine


def unrotate(g, cosine, sine):
    return g * cosine - pltpu.roll(g, HALF, 1) * sine


def views(meta, refs):
    if len(refs) == 1:
        return [(refs[0].at[i], i) for i in range(refs[0].shape[0])]
    return [(ref, jnp.bitwise_xor(meta[0], k)) for k, ref in enumerate(refs)]


def start_of(index, size):
    return pl.ds(index * size if isinstance(index, int) else pl.multiple_of(index * size, size), size)


def set_shapes(joined, n, shape, dtype=jnp.bfloat16):
    if joined:
        return [jax.ShapeDtypeStruct((n,) + shape, dtype)]
    return [jax.ShapeDtypeStruct(shape, dtype)] * n


def set_specs(joined, n, shape, index_map):
    if joined:
        return [pl.BlockSpec((n,) + shape, lambda *i: (0,) + index_map(*i))]
    return [pl.BlockSpec(shape, index_map)] * n


def dot(a, b, contract):
    return lax.dot_general(a, b, (contract, ((), ())), preferred_element_type=jnp.float32)


def cut_kernel(n, meta, lengths, turned, plain, *refs):
    pieces, (held, cosine, sine, sems) = refs[-4 - n : -4], refs[-4:]
    rows, width = turned.shape[0], held.shape[2]
    copies = []
    for step, piece in enumerate(pieces):
        lanes = start_of(jnp.bitwise_xor(meta[0], step), width)
        copies.append(
            (
                pltpu.make_async_copy(turned.at[:, lanes], held.at[step], sems.at[step, 0]),
                pltpu.make_async_copy(plain.at[:, lanes], piece.at[1], sems.at[step, 1]),
            )
        )
    for t in range(2):
        for step in range(n):
            copies[step][t].start()
    fill_tables(lengths, meta[1] * (rows * n) + meta[0] * rows, cosine, sine)
    for step, piece in enumerate(pieces):
        copies[step][0].wait()
        for h in range(0, width, HEAD_SIZE):
            lanes = slice(h, h + HEAD_SIZE)
            x = held[step, :, lanes].astype(jnp.float32)
            piece[0, :, lanes] = rotate(x, cosine[...], sine[...]).astype(jnp.bfloat16)
    for step in range(n):
        copies[step][1].wait()


def cut(meta, lengths, turned, plain, n, after=()):
    rows, width = turned.shape[0], turned.shape[1] // n
    return pl.pallas_call(
        functools.partial(cut_kernel, n),
        out_shape=[jax.ShapeDtypeStruct((2, rows, width), jnp.bfloat16)] * n,
        in_specs=[SMEM_SPEC] * 2 + [HBM_SPEC] * 2 + [ANY_SPEC] * len(after),
        out_specs=[VMEM_SPEC] * n,
        scratch_shapes=[
            pltpu.VMEM((n, rows, width), jnp.bfloat16),
            pltpu.VMEM((rows, HEAD_SIZE), jnp.float32),
            pltpu.VMEM((rows, HEAD_SIZE), jnp.float32),
            pltpu.SemaphoreType.DMA((n, 2)),
        ],
        compiler_params=params(WIDE_LIMIT),
        cost_estimate=cost(0, 8 * n * rows * width),
        name="cut",
    )(meta, lengths, turned, plain, *after)


def tables_kernel(meta, lengths, cosine, sine, half_cosine, half_sine):
    first = meta[1] * cosine.shape[0]
    fill_tables(lengths, first, cosine, sine, SCALE)
    angle, _ = chain_angles(lengths, first, half_cosine.shape, 1)
    half_cosine[...] = jnp.cos(angle) * SCALE
    half_sine[...] = jnp.sin(angle) * SCALE


def tables(meta, lengths, length):
    return pl.pallas_call(
        tables_kernel,
        out_shape=[jax.ShapeDtypeStruct((length, HEAD_SIZE), jnp.float32)] * 2
        + [jax.ShapeDtypeStruct((HALF, length), jnp.float32)] * 2,
        in_specs=[SMEM_SPEC] * 2,
        compiler_params=params(),
        cost_estimate=cost(0, 8 * length * HEAD_SIZE),
        name="tables",
    )(meta, lengths)


def order_kernel(meta, *refs):
    out = refs[-1]
    for piece, index in views(meta, refs[:-1]):
        out[:, start_of(index, piece.shape[1]), :] = piece[...]


def order(meta, pieces, n, after=()):
    _, rows, width = pieces[0].shape[-3:]
    return pl.pallas_call(
        behind(order_kernel, len(after)),
        grid=(1,),
        out_shape=jax.ShapeDtypeStruct((2, n * rows, width), pieces[0].dtype),
        in_specs=[ANY_SPEC] * len(after)
        + [SMEM_SPEC]
        + set_specs(len(pieces) == 1, n, (2, rows, width), lambda i: (0, 0, 0)),
        out_specs=pl.BlockSpec((2, n * rows, width), lambda i: (0, 0, 0)),
        compiler_params=params(),
        cost_estimate=cost(0, 8 * n * rows * width),
        name="order",
    )(*after, meta, *pieces)


def attend_kernel(count, heads, meta, listed, half_cosine, half_sine, low, mid, high, *refs):
    inputs, results = views(meta, refs[:count]), views(meta, refs[count:-7])
    lower, upper, own, query_s, grad_s, out_s, back_s = refs[-7:]
    length = mid.shape[1]
    nblk = length // BLOCK_TOKENS
    for piece, index in inputs:
        place = start_of(index, piece.shape[1])
        query_s[place, :] = piece[0]
        grad_s[place, :] = piece[1]
    first = meta[1] * nblk
    query_block = lax.broadcasted_iota(jnp.int32, (1, length), 1) // BLOCK_TOKENS
    addends = []
    for key_block in range(3 * nblk):
        addend = jnp.zeros((1, length), jnp.float32)
        for block in range(nblk):
            times = jnp.int32(0)
            for p in range(listed.shape[1]):
                same = listed[first + block, p] == first + key_block - nblk
                times += jnp.where(same & (listed[first + block, p] >= 0), 1, 0)
            addend = jnp.where(query_block == block, times.astype(jnp.float32), addend)
        addends.append(jnp.where(addend > 0, jnp.log2(jnp.maximum(addend, 1.0)), masked_score))
    for h in range(heads):
        lanes = slice(h * HEAD_SIZE, (h + 1) * HEAD_SIZE)
        query, grad = query_s[:, lanes], grad_s[:, lanes]
        scores = []
        for i, part in enumerate((low, mid, high)):
            score = dot(part[0, :, lanes], query, ((1,), (1,))) * (SCALE * math.log2(math.e))
            for b in range(nblk):
                block = score[b * BLOCK_TOKENS : (b + 1) * BLOCK_TOKENS]
                scores.append(block + addends[i * nblk + b])
        top = functools.reduce(jnp.maximum, [jnp.max(s, axis=0, keepdims=True) for s in scores])
        raised = [jnp.exp2(s - top) for s in scores]
        total = sum(jnp.sum(r, axis=0, keepdims=True) for r in raised)
        scaling = 1.0 / total
        delta = jnp.zeros((1, length), jnp.float32)
        out = jnp.zeros((HEAD_SIZE, length), jnp.float32)
        chances, grad_chances = [], []
        for i, (part, sums) in enumerate(((low, lower), (mid, own), (high, upper))):
            chance = jnp.concatenate(raised[i * nblk : (i + 1) * nblk], axis=0) * scaling
            weights = chance.astype(jnp.bfloat16)
            sums[1, :, lanes] = dot(weights, grad, ((1,), (0,))).astype(sums.dtype)
            out += dot(part[1, :, lanes], weights, ((0,), (0,)))
            grad_chance = dot(part[1, :, lanes], grad, ((1,), (1,)))
            delta += jnp.sum(chance * grad_chance, axis=0, keepdims=True)
            chances.append(chance)
            grad_chances.append(grad_chance)
        back = jnp.zeros((HEAD_SIZE, length), jnp.float32)
        for i, (part, sums) in enumerate(((low, lower), (mid, own), (high, upper))):
            grad_score = (chances[i] * (grad_chances[i] - delta)).astype(jnp.bfloat16)
            sums[0, :, lanes] = dot(grad_score, query, ((1,), (0,))).astype(sums.dtype)
            back += dot(part[0, :, lanes], grad_score, ((0,), (0,)))
        near, far = back[:HALF], back[HALF:]
        back = jnp.concatenate(
            [
                near * half_cosine[...] + far * half_sine[...],
                far * half_cosine[...] - near * half_sine[...],
            ],
            axis=0,
        )
        out_s[:, lanes] = out.T.astype(jnp.bfloat16)
        back_s[:, lanes] = back.T.astype(jnp.bfloat16)
    for result, index in results:
        place = start_of(index, result.shape[1])
        result[0] = out_s[place, :]
        result[1] = back_s[place, :]


def attend(meta, listed, half_cosine, half_sine, low, mid, high, inputs, n, joined, heads, after=()):
    _, length, width = mid.shape
    rows, lanes = length // n, heads * HEAD_SIZE
    window = pl.BlockSpec((2, length, lanes), lambda i: (0, 0, i))
    sources = set_specs(len(inputs) == 1, n, (2, rows, lanes), lambda i: (0, 0, i))
    targets = set_specs(joined, n, (2, rows, lanes), lambda i: (0, 0, i))
    table = pl.BlockSpec(half_cosine.shape, lambda i: (0, 0))
    results = pl.pallas_call(
        behind(functools.partial(attend_kernel, len(inputs), heads), len(after)),
        grid=(width // lanes,),
        out_shape=set_shapes(joined, n, (2, rows, width))
        + [jax.ShapeDtypeStruct(mid.shape, jnp.bfloat16)] * 2
        + [jax.ShapeDtypeStruct(mid.shape, jnp.float32)],
        in_specs=[ANY_SPEC] * len(after)
        + [SMEM_SPEC, SMEM_SPEC, table, table]
        + [window] * 3
        + sources,
        out_specs=targets + [window] * 3,
        scratch_shapes=[pltpu.VMEM((length, lanes), jnp.bfloat16)] * 4,
        compiler_params=params(),
        cost_estimate=cost(36 * length * length * width, 40 * length * width),
        name="attend",
    )(*after, meta, listed, half_cosine, half_sine, low, mid, high, *inputs)
    return results[:-3], *results[-3:]


def combine_kernel(meta, cosine, sine, own, from_upper, from_lower, *pieces):
    for piece, index in views(meta, pieces):
        place = start_of(index, piece.shape[1])
        for h in range(0, own.shape[2], HEAD_SIZE):
            lanes = slice(h, h + HEAD_SIZE)
            for t in range(2):
                total = (
                    own[t, place, lanes]
                    + from_upper[t, place, lanes].astype(jnp.float32)
                    + from_lower[t, place, lanes].astype(jnp.float32)
                )
                if t == 0:
                    total = unrotate(total, cosine[place, :], sine[place, :])
                piece[t, :, lanes] = total.astype(jnp.bfloat16)


def combine(meta, cosine, sine, own, from_upper, from_lower, n):
    _, length, width = own.shape
    return pl.pallas_call(
        combine_kernel,
        out_shape=[jax.ShapeDtypeStruct((2, length // n, width), jnp.bfloat16)] * n,
        in_specs=[SMEM_SPEC] + [VMEM_SPEC] * 5,
        out_specs=[VMEM_SPEC] * n,
        compiler_params=params(),
        cost_estimate=cost(0, 20 * length * width),
        name="combine",
    )(meta, cosine, sine, own, from_upper, from_lower)


def join_kernel(n, meta, *refs):
    pieces, outs, sems = refs[:n], refs[n:-1], refs[-1]
    copies = []
    for step, piece in enumerate(pieces):
        lanes = start_of(jnp.bitwise_xor(meta[0], step), piece.shape[2])
        for t, out in enumerate(outs):
            copies.append(pltpu.make_async_copy(piece.at[t], out.at[:, lanes], sems.at[step, t]))
    for copy in copies:
        copy.start()
    for copy in copies:
        copy.wait()


def join(meta, pieces):
    n = len(pieces)
    count, rows, width = pieces[0].shape
    return pl.pallas_call(
        functools.partial(join_kernel, n),
        out_shape=[jax.ShapeDtypeStruct((rows, n * width), jnp.bfloat16)] * count,
        in_specs=[SMEM_SPEC] + [ANY_SPEC] * n,
        out_specs=[HBM_SPEC] * count,
        scratch_shapes=[pltpu.SemaphoreType.DMA((n, count))],
        compiler_params=params(),
        cost_estimate=cost(0, 4 * n * count * rows * width),
        name="join",
    )(meta, *pieces)


def swap(pieces):
    if len(pieces) == 1:
        return [lax.all_to_all(pieces[0], "head", 0, 0, tiled=True)]
    n = len(pieces)
    return [pieces[0]] + [
        lax.ppermute(pieces[k], "head", [(i, i ^ k) for i in range(n)]) for k in range(1, n)
    ]


def shift(block, distance):
    devices = range(lax.axis_size("seq"))
    return lax.ppermute(block, "seq", [(i, i + distance) for i in devices if i + distance in devices])


def on_device(queries, keys, values, out_grad, chain_lengths, block_pairs):
    n = lax.axis_size("head")
    length = queries.shape[0] * n
    meta = jnp.stack([lax.axis_index("head"), lax.axis_index("seq")]).astype(jnp.int32)
    cosine, sine, half_cosine, half_sine = tables(meta, chain_lengths, length)

    key_value = swap(cut(meta, chain_lengths, keys, values, n))
    later = cut(meta, chain_lengths, queries, out_grad, n, [key_value[1], cosine])
    inputs = swap(later)
    mid = order(meta, key_value, n, [later[0]])
    low, high = shift(mid, 1), shift(mid, -1)
    results, lower, upper, own = attend(
        meta, block_pairs, half_cosine, half_sine, low, mid, high, inputs, n, False, 5
    )
    attn_out, query_grad = join(meta, swap(results))
    from_upper, from_lower = shift(lower, -1), shift(upper, 1)
    back = swap(combine(meta, cosine, sine, own, from_upper, from_lower, n))
    key_grad, value_grad = join(meta, back)
    return attn_out, query_grad, key_grad, value_grad


def solution(mesh):
    split = P(("seq", "head"), None)
    return jax.shard_map(
        on_device,
        mesh=mesh,
        in_specs=(split, split, split, split, P(), P()),
        out_specs=(split, split, split, split),
        check_vma=False,
    )
```

```python
import functools
import math

import jax
import jax.numpy as jnp
from jax import lax
from jax.experimental import pallas as pl
from jax.experimental.pallas import tpu as pltpu
from jax.sharding import PartitionSpec as P

HEAD_SIZE = 128
BLOCK_TOKENS = 128
HALF = HEAD_SIZE // 2
SCALE = 1.0 / math.sqrt(HEAD_SIZE)
VMEM_LIMIT = 32 * 1024 * 1024
WIDE_LIMIT = 60 * 1024 * 1024
PARTS = 1

masked_score = -1e30
rotary_base = 10000.0

SMEM_SPEC = pl.BlockSpec(memory_space=pltpu.SMEM)


def cost(flops, moved, exps=0):
    return pl.CostEstimate(flops=flops, bytes_accessed=moved, transcendentals=exps)


def params(limit=VMEM_LIMIT):
    return pltpu.CompilerParams(vmem_limit_bytes=limit)


def behind(kernel, count):
    def run(*refs):
        kernel(*refs[count:])

    return run if count else kernel


ANY_SPEC = pl.BlockSpec(memory_space=pl.ANY)
HBM_SPEC = pl.BlockSpec(memory_space=pltpu.HBM)
VMEM_SPEC = pl.BlockSpec(memory_space=pltpu.VMEM)


def chain_angles(lengths, first_row, shape, tokens):
    row = first_row + lax.broadcasted_iota(jnp.int32, shape, tokens)

    def look(c, carry):
        start, begin = carry
        return start + lengths[c], jnp.maximum(begin, jnp.where(row >= start, start, 0))

    _, begin = lax.fori_loop(
        0, lengths.shape[0], look, (jnp.int32(0), jnp.zeros(shape, jnp.int32))
    )
    entry = lax.broadcasted_iota(jnp.int32, shape, 1 - tokens)
    column = jnp.where(entry < HALF, entry, entry - HALF).astype(jnp.float32)
    frequency = jnp.exp(column * (-2.0 * math.log(rotary_base) / HEAD_SIZE))
    return (row - begin).astype(jnp.float32) * frequency, entry


def fill_tables(lengths, first_row, cosine, sine):
    angle, entry = chain_angles(lengths, first_row, cosine.shape, 0)
    turn = jnp.sin(angle)
    cosine[...] = jnp.cos(angle)
    sine[...] = jnp.where(entry < HALF, -turn, turn)


def rotate(x, cosine, sine):
    return x * cosine + pltpu.roll(x, HALF, 1) * sine


def unrotate(g, cosine, sine):
    return g * cosine - pltpu.roll(g, HALF, 1) * sine


def views(meta, refs):
    if len(refs) == 1:
        return [(refs[0].at[i], i) for i in range(refs[0].shape[0])]
    return [(ref, jnp.bitwise_xor(meta[0], k)) for k, ref in enumerate(refs)]


def start_of(index, size):
    return pl.ds(index * size if isinstance(index, int) else pl.multiple_of(index * size, size), size)


def set_shapes(joined, n, shape, dtype=jnp.bfloat16):
    if joined:
        return [jax.ShapeDtypeStruct((n,) + shape, dtype)]
    return [jax.ShapeDtypeStruct(shape, dtype)] * n


def set_specs(joined, n, shape, index_map):
    if joined:
        return [pl.BlockSpec((n,) + shape, lambda *i: (0,) + index_map(*i))]
    return [pl.BlockSpec(shape, index_map)] * n


def dot(a, b, contract):
    return lax.dot_general(a, b, (contract, ((), ())), preferred_element_type=jnp.float32)


def cut_kernel(n, offset, meta, lengths, turned, plain, *refs):
    pieces, (held, cosine, sine, sems) = refs[-4 - n : -4], refs[-4:]
    rows, width = turned.shape[0], held.shape[2]
    copies = []
    for step, piece in enumerate(pieces):
        base = jnp.bitwise_xor(meta[0], step) * (turned.shape[1] // n) + offset
        lanes = pl.ds(pl.multiple_of(base, HEAD_SIZE), width)
        copies.append(
            (
                pltpu.make_async_copy(turned.at[:, lanes], held.at[step], sems.at[step, 0]),
                pltpu.make_async_copy(plain.at[:, lanes], piece.at[1], sems.at[step, 1]),
            )
        )
    for t in range(2):
        for step in range(n):
            copies[step][t].start()
    fill_tables(lengths, meta[1] * (rows * n) + meta[0] * rows, cosine, sine)
    for step, piece in enumerate(pieces):
        copies[step][0].wait()
        for h in range(0, width, HEAD_SIZE):
            lanes = slice(h, h + HEAD_SIZE)
            x = held[step, :, lanes].astype(jnp.float32)
            piece[0, :, lanes] = rotate(x, cosine[...], sine[...]).astype(jnp.bfloat16)
    for step in range(n):
        copies[step][1].wait()


def cut(meta, lengths, turned, plain, n, limit, part=0, parts=1, after=()):
    rows, width = turned.shape[0], turned.shape[1] // (n * parts)
    return pl.pallas_call(
        functools.partial(cut_kernel, n, part * width),
        out_shape=[jax.ShapeDtypeStruct((2, rows, width), jnp.bfloat16)] * n,
        in_specs=[SMEM_SPEC] * 2 + [HBM_SPEC] * 2 + [ANY_SPEC] * len(after),
        out_specs=[VMEM_SPEC] * n,
        scratch_shapes=[
            pltpu.VMEM((n, rows, width), jnp.bfloat16),
            pltpu.VMEM((rows, HEAD_SIZE), jnp.float32),
            pltpu.VMEM((rows, HEAD_SIZE), jnp.float32),
            pltpu.SemaphoreType.DMA((n, 2)),
        ],
        compiler_params=params(limit),
        cost_estimate=cost(0, 8 * n * rows * width),
        name="cut",
    )(meta, lengths, turned, plain, *after)


def tables_kernel(meta, lengths, cosine, sine, half_cosine, half_sine):
    first = meta[1] * cosine.shape[0]
    fill_tables(lengths, first, cosine, sine)
    angle, _ = chain_angles(lengths, first, half_cosine.shape, 1)
    half_cosine[...] = jnp.cos(angle)
    half_sine[...] = jnp.sin(angle)


def tables(meta, lengths, length, after):
    return pl.pallas_call(
        behind(tables_kernel, len(after)),
        out_shape=[jax.ShapeDtypeStruct((length, HEAD_SIZE), jnp.float32)] * 2
        + [jax.ShapeDtypeStruct((HALF, length), jnp.float32)] * 2,
        in_specs=[ANY_SPEC] * len(after) + [SMEM_SPEC] * 2,
        compiler_params=params(),
        cost_estimate=cost(0, 8 * length * HEAD_SIZE),
        name="tables",
    )(*after, meta, lengths)


def order_kernel(n, meta, *refs):
    outs = refs[n:]
    width = outs[0].shape[2]
    for piece, index in views(meta, refs[:n]):
        for part, out in enumerate(outs):
            out[:, start_of(index, piece.shape[1]), :] = piece[:, :, part * width : (part + 1) * width]


def order(meta, pieces, parts, after=()):
    _, rows, width = pieces[0].shape
    n = len(pieces)
    shape = jax.ShapeDtypeStruct((2, n * rows, width // parts), jnp.bfloat16)
    return pl.pallas_call(
        behind(functools.partial(order_kernel, n), len(after)),
        out_shape=[shape] * parts,
        in_specs=[ANY_SPEC] * len(after) + [SMEM_SPEC] + [VMEM_SPEC] * n,
        out_specs=[VMEM_SPEC] * parts,
        compiler_params=params(),
        cost_estimate=cost(0, 8 * n * rows * width),
        name="order",
    )(*after, meta, *pieces)


def window_shards(shard):
    odd = lax.rem(shard, 2)
    return shard, shard + 1 - 2 * odd, shard - 1 + 2 * odd


def attend_kernel(count, heads, meta, listed, half_cosine, half_sine, mid, near, far, *refs):
    inputs, results = views(meta, refs[:count]), views(meta, refs[count:-7])
    own, near_sum, far_sum, query_s, grad_s, out_s, back_s = refs[-7:]
    length = mid.shape[1]
    nblk = length // BLOCK_TOKENS
    for piece, index in inputs:
        place = start_of(index, piece.shape[1])
        query_s[place, :] = piece[0]
        grad_s[place, :] = piece[1]
    first = meta[1] * nblk
    query_block = lax.broadcasted_iota(jnp.int32, (1, length), 1) // BLOCK_TOKENS
    addends = []
    for shard in window_shards(meta[1]):
        for key_block in range(nblk):
            addend = jnp.zeros((1, length), jnp.float32)
            for block in range(nblk):
                times = jnp.int32(0)
                for p in range(listed.shape[1]):
                    entry = listed[first + block, p]
                    times += jnp.where((entry >= 0) & (entry == shard * nblk + key_block), 1, 0)
                addend = jnp.where(query_block == block, times.astype(jnp.float32), addend)
            addends.append(jnp.where(addend > 0, jnp.log2(jnp.maximum(addend, 1.0)), masked_score))
    window = ((mid, own), (near, near_sum), (far, far_sum))
    for h in range(heads):
        lanes = slice(h * HEAD_SIZE, (h + 1) * HEAD_SIZE)
        query, grad = query_s[:, lanes], grad_s[:, lanes]
        scores = []
        for i, part in enumerate((mid, near, far)):
            score = dot(part[0, :, lanes], query, ((1,), (1,))) * (SCALE * math.log2(math.e))
            for b in range(nblk):
                block = score[b * BLOCK_TOKENS : (b + 1) * BLOCK_TOKENS]
                scores.append(block + addends[i * nblk + b])
        top = functools.reduce(jnp.maximum, [jnp.max(s, axis=0, keepdims=True) for s in scores])
        raised = [jnp.exp2(s - top) for s in scores]
        total = sum(jnp.sum(r, axis=0, keepdims=True) for r in raised)
        scaling = 1.0 / total
        delta = jnp.zeros((1, length), jnp.float32)
        out = jnp.zeros((HEAD_SIZE, length), jnp.float32)
        chances, grad_chances = [], []
        for i, (part, sums) in enumerate(window):
            chance = jnp.concatenate(raised[i * nblk : (i + 1) * nblk], axis=0) * scaling
            weights = chance.astype(jnp.bfloat16)
            sums[1, :, lanes] = dot(weights, grad, ((1,), (0,))).astype(sums.dtype)
            out += dot(part[1, :, lanes], weights, ((0,), (0,)))
            grad_chance = dot(part[1, :, lanes], grad, ((1,), (1,)))
            delta += jnp.sum(chance * grad_chance, axis=0, keepdims=True)
            chances.append(chance)
            grad_chances.append(grad_chance)
        back = jnp.zeros((HEAD_SIZE, length), jnp.float32)
        for i, (part, sums) in enumerate(window):
            grad_score = (chances[i] * (grad_chances[i] - delta) * SCALE).astype(jnp.bfloat16)
            sums[0, :, lanes] = dot(grad_score, query, ((1,), (0,))).astype(sums.dtype)
            back += dot(part[0, :, lanes], grad_score, ((0,), (0,)))
        low, high = back[:HALF], back[HALF:]
        back = jnp.concatenate(
            [
                low * half_cosine[...] + high * half_sine[...],
                high * half_cosine[...] - low * half_sine[...],
            ],
            axis=0,
        )
        out_s[:, lanes] = out.T.astype(jnp.bfloat16)
        back_s[:, lanes] = back.T.astype(jnp.bfloat16)
    for result, index in results:
        place = start_of(index, result.shape[1])
        result[0] = out_s[place, :]
        result[1] = back_s[place, :]


def attend(meta, listed, half_cosine, half_sine, mid, near, far, inputs, part, parts, before):
    n = len(inputs)
    _, length, width = mid.shape
    rows, whole = length // n, width * parts
    window = pl.BlockSpec(mid.shape, lambda i: (0, 0, 0))
    sums = pl.BlockSpec(mid.shape, lambda i: (0, 0, part))
    source = pl.BlockSpec((2, rows, width), lambda i: (0, 0, 0))
    target = pl.BlockSpec((2, rows, width), lambda i: (0, 0, part))
    table = pl.BlockSpec(half_cosine.shape, lambda i: (0, 0))
    results = pl.pallas_call(
        behind(functools.partial(attend_kernel, n, width // HEAD_SIZE), len(before)),
        grid=(1,),
        out_shape=[jax.ShapeDtypeStruct((2, rows, whole), jnp.bfloat16)] * n
        + [jax.ShapeDtypeStruct((2, length, whole), jnp.float32)]
        + [jax.ShapeDtypeStruct((2, length, whole), jnp.bfloat16)] * 2,
        in_specs=[ANY_SPEC] * len(before)
        + [SMEM_SPEC, SMEM_SPEC, table, table]
        + [window] * 3
        + [source] * n,
        out_specs=[target] * n + [sums] * 3,
        scratch_shapes=[pltpu.VMEM((length, width), jnp.bfloat16)] * 4,
        input_output_aliases={t: t for t in range(len(before))},
        compiler_params=params(),
        cost_estimate=cost(36 * length * length * width, 40 * length * width),
        name="attend",
    )(*before, meta, listed, half_cosine, half_sine, mid, near, far, *inputs)
    return results


def combine_kernel(meta, cosine, sine, own, from_near, from_far, *pieces):
    for piece, index in views(meta, pieces):
        place = start_of(index, piece.shape[1])
        for h in range(0, own.shape[2], HEAD_SIZE):
            lanes = slice(h, h + HEAD_SIZE)
            for t in range(2):
                total = (
                    own[t, place, lanes]
                    + from_near[t, place, lanes].astype(jnp.float32)
                    + from_far[t, place, lanes].astype(jnp.float32)
                )
                if t == 0:
                    total = unrotate(total, cosine[place, :], sine[place, :])
                piece[t, :, lanes] = total.astype(jnp.bfloat16)


def combine(meta, cosine, sine, own, from_near, from_far, n):
    _, length, width = own.shape
    return pl.pallas_call(
        combine_kernel,
        out_shape=[jax.ShapeDtypeStruct((2, length // n, width), jnp.bfloat16)] * n,
        in_specs=[SMEM_SPEC] + [VMEM_SPEC] * 5,
        out_specs=[VMEM_SPEC] * n,
        compiler_params=params(),
        cost_estimate=cost(0, 20 * length * width),
        name="combine",
    )(meta, cosine, sine, own, from_near, from_far)


def join_kernel(n, meta, *refs):
    pieces, outs, sems = refs[:n], refs[n:-1], refs[-1]
    copies = []
    for step, piece in enumerate(pieces):
        lanes = start_of(jnp.bitwise_xor(meta[0], step), piece.shape[2])
        for t, out in enumerate(outs):
            copies.append(pltpu.make_async_copy(piece.at[t], out.at[:, lanes], sems.at[step, t]))
    for copy in copies:
        copy.start()
    for copy in copies:
        copy.wait()


def join(meta, pieces):
    n = len(pieces)
    count, rows, width = pieces[0].shape
    return pl.pallas_call(
        functools.partial(join_kernel, n),
        out_shape=[jax.ShapeDtypeStruct((rows, n * width), jnp.bfloat16)] * count,
        in_specs=[SMEM_SPEC] + [ANY_SPEC] * n,
        out_specs=[HBM_SPEC] * count,
        scratch_shapes=[pltpu.SemaphoreType.DMA((n, count))],
        compiler_params=params(),
        cost_estimate=cost(0, 4 * n * count * rows * width),
        name="join",
    )(meta, *pieces)


def swap(pieces):
    if len(pieces) == 1:
        return [lax.all_to_all(pieces[0], "head", 0, 0, tiled=True)]
    n = len(pieces)
    return [pieces[0]] + [
        lax.ppermute(pieces[k], "head", [(i, i ^ k) for i in range(n)]) for k in range(1, n)
    ]


def trade(block, first):
    route = []
    for i in range(first, lax.axis_size("seq") - 1, 2):
        route += [(i, i + 1), (i + 1, i)]
    return lax.ppermute(block, "seq", route)


def on_device(queries, keys, values, out_grad, chain_lengths, block_pairs):
    n = lax.axis_size("head")
    length = queries.shape[0] * n
    meta = jnp.stack([lax.axis_index("head"), lax.axis_index("seq")]).astype(jnp.int32)
    key_value = swap(cut(meta, chain_lengths, keys, values, n, WIDE_LIMIT))
    laters = [
        cut(meta, chain_lengths, queries, out_grad, n, VMEM_LIMIT, part, PARTS, [key_value[1]])
        for part in range(PARTS)
    ]
    inputs = [swap(later) for later in laters]
    mids = order(meta, key_value, PARTS, [later[0] for later in laters])
    nears, fars = [trade(mid, 0) for mid in mids], [trade(mid, 1) for mid in mids]
    cosine, sine, half_cosine, half_sine = tables(meta, chain_lengths, length, [inputs[0][1]])
    sums = []
    for part in range(PARTS):
        sums = attend(
            meta,
            block_pairs,
            half_cosine,
            half_sine,
            mids[part],
            nears[part],
            fars[part],
            inputs[part],
            part,
            PARTS,
            sums,
        )
    results, (own, near_sum, far_sum) = sums[:n], sums[n:]
    attn_out, query_grad = join(meta, swap(results))
    from_near, from_far = trade(near_sum, 0), trade(far_sum, 1)
    back = swap(combine(meta, cosine, sine, own, from_near, from_far, n))
    key_grad, value_grad = join(meta, back)
    return attn_out, query_grad, key_grad, value_grad


def solution(mesh):
    split = P(("seq", "head"), None)
    return jax.shard_map(
        on_device,
        mesh=mesh,
        in_specs=(split, split, split, split, P(), P()),
        out_specs=(split, split, split, split),
        check_vma=False,
    )
```

```python
import functools
import math

import jax
import jax.numpy as jnp
from jax import lax
from jax.experimental import pallas as pl
from jax.experimental.pallas import tpu as pltpu
from jax.sharding import PartitionSpec as P

HEAD_SIZE = 128
BLOCK_TOKENS = 128
HALF = HEAD_SIZE // 2
SCALE = 1.0 / math.sqrt(HEAD_SIZE)
VMEM_LIMIT = 32 * 1024 * 1024
WIDE_LIMIT = 60 * 1024 * 1024
HEADS_A_STEP = 10

masked_score = -1e30
rotary_base = 10000.0

SMEM_SPEC = pl.BlockSpec(memory_space=pltpu.SMEM)


def cost(flops, moved, exps=0):
    return pl.CostEstimate(flops=flops, bytes_accessed=moved, transcendentals=exps)


def params(limit=VMEM_LIMIT):
    return pltpu.CompilerParams(vmem_limit_bytes=limit)


def behind(kernel, count):
    def run(*refs):
        kernel(*refs[count:])

    return run if count else kernel


ANY_SPEC = pl.BlockSpec(memory_space=pl.ANY)
HBM_SPEC = pl.BlockSpec(memory_space=pltpu.HBM)
VMEM_SPEC = pl.BlockSpec(memory_space=pltpu.VMEM)


def chain_angles(lengths, first_row, shape, tokens):
    row = first_row + lax.broadcasted_iota(jnp.int32, shape, tokens)

    def look(c, carry):
        start, begin = carry
        return start + lengths[c], jnp.maximum(begin, jnp.where(row >= start, start, 0))

    _, begin = lax.fori_loop(
        0, lengths.shape[0], look, (jnp.int32(0), jnp.zeros(shape, jnp.int32))
    )
    entry = lax.broadcasted_iota(jnp.int32, shape, 1 - tokens)
    column = jnp.where(entry < HALF, entry, entry - HALF).astype(jnp.float32)
    frequency = jnp.exp(column * (-2.0 * math.log(rotary_base) / HEAD_SIZE))
    return (row - begin).astype(jnp.float32) * frequency, entry


def fill_tables(lengths, first_row, cosine, sine):
    angle, entry = chain_angles(lengths, first_row, cosine.shape, 0)
    turn = jnp.sin(angle)
    cosine[...] = jnp.cos(angle)
    sine[...] = jnp.where(entry < HALF, -turn, turn)


def rotate(x, cosine, sine):
    return x * cosine + pltpu.roll(x, HALF, 1) * sine


def unrotate(g, cosine, sine):
    return g * cosine - pltpu.roll(g, HALF, 1) * sine


def views(meta, refs):
    if len(refs) == 1:
        return [(refs[0].at[i], i) for i in range(refs[0].shape[0])]
    return [(ref, jnp.bitwise_xor(meta[0], k)) for k, ref in enumerate(refs)]


def start_of(index, size):
    return pl.ds(index * size if isinstance(index, int) else pl.multiple_of(index * size, size), size)


def set_shapes(joined, n, shape, dtype=jnp.bfloat16):
    if joined:
        return [jax.ShapeDtypeStruct((n,) + shape, dtype)]
    return [jax.ShapeDtypeStruct(shape, dtype)] * n


def set_specs(joined, n, shape, index_map):
    if joined:
        return [pl.BlockSpec((n,) + shape, lambda *i: (0,) + index_map(*i))]
    return [pl.BlockSpec(shape, index_map)] * n


def dot(a, b, contract):
    return lax.dot_general(a, b, (contract, ((), ())), preferred_element_type=jnp.float32)


def cut_kernel(n, meta, lengths, turned, plain, *refs):
    pieces, (held, cosine, sine, sems) = refs[-4 - n : -4], refs[-4:]
    rows, width = turned.shape[0], held.shape[2]
    copies = []
    for step, piece in enumerate(pieces):
        lanes = start_of(jnp.bitwise_xor(meta[0], step), width)
        copies.append(
            (
                pltpu.make_async_copy(turned.at[:, lanes], held.at[step], sems.at[step, 0]),
                pltpu.make_async_copy(plain.at[:, lanes], piece.at[1], sems.at[step, 1]),
            )
        )
    for t in range(2):
        for step in range(n):
            copies[step][t].start()
    fill_tables(lengths, meta[1] * (rows * n) + meta[0] * rows, cosine, sine)
    for step, piece in enumerate(pieces):
        copies[step][0].wait()
        for h in range(0, width, HEAD_SIZE):
            lanes = slice(h, h + HEAD_SIZE)
            x = held[step, :, lanes].astype(jnp.float32)
            piece[0, :, lanes] = rotate(x, cosine[...], sine[...]).astype(jnp.bfloat16)
    for step in range(n):
        copies[step][1].wait()


def cut(meta, lengths, turned, plain, n, limit, after=()):
    rows, width = turned.shape[0], turned.shape[1] // n
    return pl.pallas_call(
        functools.partial(cut_kernel, n),
        out_shape=[jax.ShapeDtypeStruct((2, rows, width), jnp.bfloat16)] * n,
        in_specs=[SMEM_SPEC] * 2 + [HBM_SPEC] * 2 + [ANY_SPEC] * len(after),
        out_specs=[VMEM_SPEC] * n,
        scratch_shapes=[
            pltpu.VMEM((n, rows, width), jnp.bfloat16),
            pltpu.VMEM((rows, HEAD_SIZE), jnp.float32),
            pltpu.VMEM((rows, HEAD_SIZE), jnp.float32),
            pltpu.SemaphoreType.DMA((n, 2)),
        ],
        compiler_params=params(limit),
        cost_estimate=cost(0, 8 * n * rows * width),
        name="cut",
    )(meta, lengths, turned, plain, *after)


def tables_kernel(meta, lengths, cosine, sine, half_cosine, half_sine):
    first = meta[1] * cosine.shape[0]
    fill_tables(lengths, first, cosine, sine)
    angle, _ = chain_angles(lengths, first, half_cosine.shape, 1)
    half_cosine[...] = jnp.cos(angle)
    half_sine[...] = jnp.sin(angle)


def tables(meta, lengths, length, after):
    return pl.pallas_call(
        behind(tables_kernel, len(after)),
        out_shape=[jax.ShapeDtypeStruct((length, HEAD_SIZE), jnp.float32)] * 2
        + [jax.ShapeDtypeStruct((HALF, length), jnp.float32)] * 2,
        in_specs=[ANY_SPEC] * len(after) + [SMEM_SPEC] * 2,
        compiler_params=params(),
        cost_estimate=cost(0, 8 * length * HEAD_SIZE),
        name="tables",
    )(*after, meta, lengths)


def order_kernel(meta, *refs):
    out = refs[-1]
    for piece, index in views(meta, refs[:-1]):
        out[:, start_of(index, piece.shape[1]), :] = piece[...]


def order(meta, pieces, after=()):
    _, rows, width = pieces[0].shape
    n = len(pieces)
    return pl.pallas_call(
        behind(order_kernel, len(after)),
        out_shape=jax.ShapeDtypeStruct((2, n * rows, width), jnp.bfloat16),
        in_specs=[ANY_SPEC] * len(after) + [SMEM_SPEC] + [VMEM_SPEC] * n,
        out_specs=VMEM_SPEC,
        compiler_params=params(),
        cost_estimate=cost(0, 8 * n * rows * width),
        name="order",
    )(*after, meta, *pieces)


def window_shards(shard):
    odd = lax.rem(shard, 2)
    return shard, shard + 1 - 2 * odd, shard - 1 + 2 * odd


def attend_kernel(count, heads, meta, listed, half_cosine, half_sine, mid, near, far, *refs):
    inputs, results = views(meta, refs[:count]), views(meta, refs[count:-7])
    own, near_sum, far_sum, query_s, grad_s, out_s, back_s = refs[-7:]
    length = mid.shape[1]
    nblk = length // BLOCK_TOKENS
    for piece, index in inputs:
        place = start_of(index, piece.shape[1])
        query_s[place, :] = piece[0]
        grad_s[place, :] = piece[1]
    first = meta[1] * nblk
    query_block = lax.broadcasted_iota(jnp.int32, (1, length), 1) // BLOCK_TOKENS
    addends = []
    for shard in window_shards(meta[1]):
        for key_block in range(nblk):
            addend = jnp.zeros((1, length), jnp.float32)
            for block in range(nblk):
                times = jnp.int32(0)
                for p in range(listed.shape[1]):
                    entry = listed[first + block, p]
                    times += jnp.where((entry >= 0) & (entry == shard * nblk + key_block), 1, 0)
                addend = jnp.where(query_block == block, times.astype(jnp.float32), addend)
            addends.append(jnp.where(addend > 0, jnp.log2(jnp.maximum(addend, 1.0)), masked_score))
    window = ((mid, own), (near, near_sum), (far, far_sum))
    def lanes_of(h):
        return slice(h * HEAD_SIZE, (h + 1) * HEAD_SIZE)

    def stage_scores(h):
        lanes, scores = lanes_of(h), []
        for i, (part, _) in enumerate(window):
            score = dot(part[0, :, lanes], query_s[:, lanes], ((1,), (1,))) * (SCALE * math.log2(math.e))
            for b in range(nblk):
                block = score[b * BLOCK_TOKENS : (b + 1) * BLOCK_TOKENS]
                scores.append(block + addends[i * nblk + b])
        return scores

    def stage_grad(h):
        lanes = lanes_of(h)
        return [dot(part[1, :, lanes], grad_s[:, lanes], ((1,), (1,))) for part, _ in window]

    def stage_soft(scores):
        top = functools.reduce(jnp.maximum, [jnp.max(s, axis=0, keepdims=True) for s in scores])
        raised = [jnp.exp2(s - top) for s in scores]
        scaling = 1.0 / sum(jnp.sum(r, axis=0, keepdims=True) for r in raised)
        return [jnp.concatenate(raised[i * nblk : (i + 1) * nblk], axis=0) * scaling for i in range(3)]

    def stage_out(h, chances):
        lanes = lanes_of(h)
        out = jnp.zeros((HEAD_SIZE, length), jnp.float32)
        for (part, sums), chance in zip(window, chances):
            weights = chance.astype(jnp.bfloat16)
            sums[1, :, lanes] = dot(weights, grad_s[:, lanes], ((1,), (0,))).astype(sums.dtype)
            out += dot(part[1, :, lanes], weights, ((0,), (0,)))
        out_s[:, lanes] = out.T.astype(jnp.bfloat16)

    def stage_back(h, chances, grad_chances):
        lanes = lanes_of(h)
        delta = sum(jnp.sum(c * g, axis=0, keepdims=True) for c, g in zip(chances, grad_chances))
        back = jnp.zeros((HEAD_SIZE, length), jnp.float32)
        for (part, sums), c, g in zip(window, chances, grad_chances):
            grad_score = (c * (g - delta) * SCALE).astype(jnp.bfloat16)
            sums[0, :, lanes] = dot(grad_score, query_s[:, lanes], ((1,), (0,))).astype(sums.dtype)
            back += dot(part[0, :, lanes], grad_score, ((0,), (0,)))
        low, high = back[:HALF], back[HALF:]
        back = jnp.concatenate(
            [
                low * half_cosine[...] + high * half_sine[...],
                high * half_cosine[...] - low * half_sine[...],
            ],
            axis=0,
        )
        back_s[:, lanes] = back.T.astype(jnp.bfloat16)

    scores = stage_scores(0)
    for h in range(heads):
        grad_chances = stage_grad(h)
        chances = stage_soft(scores)
        if h + 1 < heads:
            scores = stage_scores(h + 1)
        stage_out(h, chances)
        stage_back(h, chances, grad_chances)
    for result, index in results:
        place = start_of(index, result.shape[1])
        result[0] = out_s[place, :]
        result[1] = back_s[place, :]


def attend(meta, listed, half_cosine, half_sine, mid, near, far, inputs, heads):
    n = len(inputs)
    _, length, width = mid.shape
    rows, lanes = length // n, heads * HEAD_SIZE
    results = pl.pallas_call(
        functools.partial(attend_kernel, n, heads),
        out_shape=[jax.ShapeDtypeStruct((2, rows, width), jnp.bfloat16)] * n
        + [jax.ShapeDtypeStruct(mid.shape, jnp.float32)]
        + [jax.ShapeDtypeStruct(mid.shape, jnp.bfloat16)] * 2,
        in_specs=[SMEM_SPEC] * 2 + [VMEM_SPEC] * (5 + n),
        out_specs=[VMEM_SPEC] * (n + 3),
        scratch_shapes=[pltpu.VMEM((length, lanes), jnp.bfloat16)] * 4,
        compiler_params=params(),
        cost_estimate=cost(36 * length * length * width, 40 * length * width),
        name="attend",
    )(meta, listed, half_cosine, half_sine, mid, near, far, *inputs)
    return results[:n], *results[n:]


def combine_kernel(meta, cosine, sine, own, from_near, from_far, *pieces):
    for piece, index in views(meta, pieces):
        place = start_of(index, piece.shape[1])
        for h in range(0, own.shape[2], HEAD_SIZE):
            lanes = slice(h, h + HEAD_SIZE)
            for t in range(2):
                total = (
                    own[t, place, lanes]
                    + from_near[t, place, lanes].astype(jnp.float32)
                    + from_far[t, place, lanes].astype(jnp.float32)
                )
                if t == 0:
                    total = unrotate(total, cosine[place, :], sine[place, :])
                piece[t, :, lanes] = total.astype(jnp.bfloat16)


def combine(meta, cosine, sine, own, from_near, from_far, n):
    _, length, width = own.shape
    return pl.pallas_call(
        combine_kernel,
        out_shape=[jax.ShapeDtypeStruct((2, length // n, width), jnp.bfloat16)] * n,
        in_specs=[SMEM_SPEC] + [VMEM_SPEC] * 5,
        out_specs=[VMEM_SPEC] * n,
        compiler_params=params(),
        cost_estimate=cost(0, 20 * length * width),
        name="combine",
    )(meta, cosine, sine, own, from_far, from_near)


def join_kernel(n, meta, *refs):
    pieces, outs, sems = refs[:n], refs[n:-1], refs[-1]
    copies = []
    for step, piece in enumerate(pieces):
        lanes = start_of(jnp.bitwise_xor(meta[0], step), piece.shape[2])
        for t, out in enumerate(outs):
            copies.append(pltpu.make_async_copy(piece.at[t], out.at[:, lanes], sems.at[step, t]))
    for copy in copies:
        copy.start()
    for copy in copies:
        copy.wait()


def join(meta, pieces):
    n = len(pieces)
    count, rows, width = pieces[0].shape
    return pl.pallas_call(
        functools.partial(join_kernel, n),
        out_shape=[jax.ShapeDtypeStruct((rows, n * width), jnp.bfloat16)] * count,
        in_specs=[SMEM_SPEC] + [ANY_SPEC] * n,
        out_specs=[HBM_SPEC] * count,
        scratch_shapes=[pltpu.SemaphoreType.DMA((n, count))],
        compiler_params=params(),
        cost_estimate=cost(0, 4 * n * count * rows * width),
        name="join",
    )(meta, *pieces)


def swap(pieces):
    if len(pieces) == 1:
        return [lax.all_to_all(pieces[0], "head", 0, 0, tiled=True)]
    n = len(pieces)
    return [pieces[0]] + [
        lax.ppermute(pieces[k], "head", [(i, i ^ k) for i in range(n)]) for k in range(1, n)
    ]


def trade(block, first):
    route = []
    for i in range(first, lax.axis_size("seq") - 1, 2):
        route += [(i, i + 1), (i + 1, i)]
    return lax.ppermute(block, "seq", route)


def on_device(queries, keys, values, out_grad, chain_lengths, block_pairs):
    n = lax.axis_size("head")
    length = queries.shape[0] * n
    meta = jnp.stack([lax.axis_index("head"), lax.axis_index("seq")]).astype(jnp.int32)
    key_value = swap(cut(meta, chain_lengths, keys, values, n, WIDE_LIMIT))
    later = cut(meta, chain_lengths, queries, out_grad, n, VMEM_LIMIT, [key_value[1]])
    inputs = swap(later)
    mid = order(meta, key_value, [later[0]])
    near, far = trade(mid, 0), trade(mid, 1)
    cosine, sine, half_cosine, half_sine = tables(meta, chain_lengths, length, [inputs[1]])
    results, own, near_sum, far_sum = attend(
        meta, block_pairs, half_cosine, half_sine, mid, near, far, inputs, HEADS_A_STEP
    )
    attn_out, query_grad = join(meta, swap(results))
    from_far, from_near = trade(far_sum, 1), trade(near_sum, 0)
    back = swap(combine(meta, cosine, sine, own, from_near, from_far, n))
    key_grad, value_grad = join(meta, back)
    return attn_out, query_grad, key_grad, value_grad


def solution(mesh):
    split = P(("seq", "head"), None)
    return jax.shard_map(
        on_device,
        mesh=mesh,
        in_specs=(split, split, split, split, P(), P()),
        out_specs=(split, split, split, split),
        check_vma=False,
    )
```

```python
import functools
import math

import jax
import jax.numpy as jnp
from jax import lax
from jax.experimental import pallas as pl
from jax.experimental.pallas import tpu as pltpu
from jax.sharding import PartitionSpec as P

HEAD_SIZE = 128
BLOCK_TOKENS = 128
HALF = HEAD_SIZE // 2
SCALE = 1.0 / math.sqrt(HEAD_SIZE)
VMEM_LIMIT = 32 * 1024 * 1024
WIDE_LIMIT = 60 * 1024 * 1024
HEADS_A_STEP = 10

masked_score = -1e30
rotary_base = 10000.0

SMEM_SPEC = pl.BlockSpec(memory_space=pltpu.SMEM)


def cost(flops, moved, exps=0):
    return pl.CostEstimate(flops=flops, bytes_accessed=moved, transcendentals=exps)


def params(limit=VMEM_LIMIT):
    return pltpu.CompilerParams(vmem_limit_bytes=limit)


def behind(kernel, count):
    def run(*refs):
        kernel(*refs[count:])

    return run if count else kernel


ANY_SPEC = pl.BlockSpec(memory_space=pl.ANY)
HBM_SPEC = pl.BlockSpec(memory_space=pltpu.HBM)
VMEM_SPEC = pl.BlockSpec(memory_space=pltpu.VMEM)


def chain_angles(lengths, first_row, shape, tokens):
    row = first_row + lax.broadcasted_iota(jnp.int32, shape, tokens)

    def look(c, carry):
        start, begin = carry
        return start + lengths[c], jnp.maximum(begin, jnp.where(row >= start, start, 0))

    _, begin = lax.fori_loop(
        0, lengths.shape[0], look, (jnp.int32(0), jnp.zeros(shape, jnp.int32))
    )
    entry = lax.broadcasted_iota(jnp.int32, shape, 1 - tokens)
    column = jnp.where(entry < HALF, entry, entry - HALF).astype(jnp.float32)
    frequency = jnp.exp(column * (-2.0 * math.log(rotary_base) / HEAD_SIZE))
    return (row - begin).astype(jnp.float32) * frequency, entry


def fill_tables(lengths, first_row, cosine, sine):
    angle, entry = chain_angles(lengths, first_row, cosine.shape, 0)
    turn = jnp.sin(angle)
    cosine[...] = jnp.cos(angle)
    sine[...] = jnp.where(entry < HALF, -turn, turn)


def rotate(x, cosine, sine):
    return x * cosine + pltpu.roll(x, HALF, 1) * sine


def unrotate(g, cosine, sine):
    return g * cosine - pltpu.roll(g, HALF, 1) * sine


def views(meta, refs):
    if len(refs) == 1:
        return [(refs[0].at[i], i) for i in range(refs[0].shape[0])]
    return [(ref, jnp.bitwise_xor(meta[0], k)) for k, ref in enumerate(refs)]


def start_of(index, size):
    return pl.ds(index * size if isinstance(index, int) else pl.multiple_of(index * size, size), size)


def set_shapes(joined, n, shape, dtype=jnp.bfloat16):
    if joined:
        return [jax.ShapeDtypeStruct((n,) + shape, dtype)]
    return [jax.ShapeDtypeStruct(shape, dtype)] * n


def set_specs(joined, n, shape, index_map):
    if joined:
        return [pl.BlockSpec((n,) + shape, lambda *i: (0,) + index_map(*i))]
    return [pl.BlockSpec(shape, index_map)] * n


def again_kernel(value, out):
    out[...] = value[...]


def again(value, after):
    return pl.pallas_call(
        behind(again_kernel, len(after)),
        out_shape=jax.ShapeDtypeStruct(value.shape, value.dtype),
        in_specs=[ANY_SPEC] * len(after) + [VMEM_SPEC],
        out_specs=VMEM_SPEC,
        compiler_params=params(),
        cost_estimate=cost(0, 2 * value.size),
        name="again",
    )(*after, value)


def dot(a, b, contract):
    return lax.dot_general(a, b, (contract, ((), ())), preferred_element_type=jnp.float32)


def cut_kernel(n, meta, lengths, turned, plain, *refs):
    pieces, (held, cosine, sine, sems) = refs[-4 - n : -4], refs[-4:]
    rows, width = turned.shape[0], held.shape[2]
    copies = []
    for step, piece in enumerate(pieces):
        lanes = start_of(jnp.bitwise_xor(meta[0], step), width)
        copies.append(
            (
                pltpu.make_async_copy(turned.at[:, lanes], held.at[step], sems.at[step, 0]),
                pltpu.make_async_copy(plain.at[:, lanes], piece.at[1], sems.at[step, 1]),
            )
        )
    for t in range(2):
        for step in range(n):
            copies[step][t].start()
    fill_tables(lengths, meta[1] * (rows * n) + meta[0] * rows, cosine, sine)
    for step, piece in enumerate(pieces):
        copies[step][0].wait()
        for h in range(0, width, HEAD_SIZE):
            lanes = slice(h, h + HEAD_SIZE)
            x = held[step, :, lanes].astype(jnp.float32)
            piece[0, :, lanes] = rotate(x, cosine[...], sine[...]).astype(jnp.bfloat16)
    for step in range(n):
        copies[step][1].wait()


def cut(meta, lengths, turned, plain, n, limit, after=()):
    rows, width = turned.shape[0], turned.shape[1] // n
    return pl.pallas_call(
        functools.partial(cut_kernel, n),
        out_shape=[jax.ShapeDtypeStruct((2, rows, width), jnp.bfloat16)] * n,
        in_specs=[SMEM_SPEC] * 2 + [HBM_SPEC] * 2 + [ANY_SPEC] * len(after),
        out_specs=[VMEM_SPEC] * n,
        scratch_shapes=[
            pltpu.VMEM((n, rows, width), jnp.bfloat16),
            pltpu.VMEM((rows, HEAD_SIZE), jnp.float32),
            pltpu.VMEM((rows, HEAD_SIZE), jnp.float32),
            pltpu.SemaphoreType.DMA((n, 2)),
        ],
        compiler_params=params(limit),
        cost_estimate=cost(0, 8 * n * rows * width),
        name="cut",
    )(meta, lengths, turned, plain, *after)


def tables_kernel(meta, lengths, cosine, sine, half_cosine, half_sine):
    first = meta[1] * cosine.shape[0]
    fill_tables(lengths, first, cosine, sine)
    angle, _ = chain_angles(lengths, first, half_cosine.shape, 1)
    half_cosine[...] = jnp.cos(angle)
    half_sine[...] = jnp.sin(angle)


def tables(meta, lengths, length, after):
    return pl.pallas_call(
        behind(tables_kernel, len(after)),
        out_shape=[jax.ShapeDtypeStruct((length, HEAD_SIZE), jnp.float32)] * 2
        + [jax.ShapeDtypeStruct((HALF, length), jnp.float32)] * 2,
        in_specs=[ANY_SPEC] * len(after) + [SMEM_SPEC] * 2,
        compiler_params=params(),
        cost_estimate=cost(0, 8 * length * HEAD_SIZE),
        name="tables",
    )(*after, meta, lengths)


def order_kernel(meta, *refs):
    out = refs[-1]
    for piece, index in views(meta, refs[:-1]):
        out[:, start_of(index, piece.shape[1]), :] = piece[...]


def order(meta, pieces, after=()):
    _, rows, width = pieces[0].shape
    n = len(pieces)
    return pl.pallas_call(
        behind(order_kernel, len(after)),
        out_shape=jax.ShapeDtypeStruct((2, n * rows, width), jnp.bfloat16),
        in_specs=[ANY_SPEC] * len(after) + [SMEM_SPEC] + [VMEM_SPEC] * n,
        out_specs=VMEM_SPEC,
        compiler_params=params(),
        cost_estimate=cost(0, 8 * n * rows * width),
        name="order",
    )(*after, meta, *pieces)


def window_shards(shard):
    odd = lax.rem(shard, 2)
    return shard, shard + 1 - 2 * odd, shard - 1 + 2 * odd


def attend_kernel(count, heads, meta, listed, half_cosine, half_sine, mid, near, far, *refs):
    inputs, results = views(meta, refs[:count]), views(meta, refs[count:-7])
    own, near_sum, far_sum, query_s, grad_s, out_s, back_s = refs[-7:]
    length = mid.shape[1]
    nblk = length // BLOCK_TOKENS
    for piece, index in inputs:
        place = start_of(index, piece.shape[1])
        query_s[place, :] = piece[0]
        grad_s[place, :] = piece[1]
    first = meta[1] * nblk
    query_block = lax.broadcasted_iota(jnp.int32, (1, length), 1) // BLOCK_TOKENS
    addends = []
    for shard in window_shards(meta[1]):
        for key_block in range(nblk):
            addend = jnp.zeros((1, length), jnp.float32)
            for block in range(nblk):
                times = jnp.int32(0)
                for p in range(listed.shape[1]):
                    entry = listed[first + block, p]
                    times += jnp.where((entry >= 0) & (entry == shard * nblk + key_block), 1, 0)
                addend = jnp.where(query_block == block, times.astype(jnp.float32), addend)
            addends.append(jnp.where(addend > 0, jnp.log2(jnp.maximum(addend, 1.0)), masked_score))
    window = ((mid, own), (near, near_sum), (far, far_sum))
    def lanes_of(h):
        return slice(h * HEAD_SIZE, (h + 1) * HEAD_SIZE)

    def stage_scores(h):
        lanes, scores = lanes_of(h), []
        for i, (part, _) in enumerate(window):
            score = dot(part[0, :, lanes], query_s[:, lanes], ((1,), (1,))) * (SCALE * math.log2(math.e))
            for b in range(nblk):
                block = score[b * BLOCK_TOKENS : (b + 1) * BLOCK_TOKENS]
                scores.append(block + addends[i * nblk + b])
        return scores

    def stage_grad(h):
        lanes = lanes_of(h)
        return [dot(part[1, :, lanes], grad_s[:, lanes], ((1,), (1,))) for part, _ in window]

    def stage_soft(scores):
        top = functools.reduce(jnp.maximum, [jnp.max(s, axis=0, keepdims=True) for s in scores])
        raised = [jnp.exp2(s - top) for s in scores]
        scaling = 1.0 / sum(jnp.sum(r, axis=0, keepdims=True) for r in raised)
        return [jnp.concatenate(raised[i * nblk : (i + 1) * nblk], axis=0) * scaling for i in range(3)]

    def stage_out(h, chances):
        lanes = lanes_of(h)
        out = jnp.zeros((HEAD_SIZE, length), jnp.float32)
        for (part, sums), chance in zip(window, chances):
            weights = chance.astype(jnp.bfloat16)
            sums[1, :, lanes] = dot(weights, grad_s[:, lanes], ((1,), (0,))).astype(sums.dtype)
            out += dot(part[1, :, lanes], weights, ((0,), (0,)))
        out_s[:, lanes] = out.T.astype(jnp.bfloat16)

    def stage_back(h, chances, grad_chances):
        lanes = lanes_of(h)
        delta = sum(jnp.sum(c * g, axis=0, keepdims=True) for c, g in zip(chances, grad_chances))
        back = jnp.zeros((HEAD_SIZE, length), jnp.float32)
        for (part, sums), c, g in zip(window, chances, grad_chances):
            grad_score = (c * (g - delta) * SCALE).astype(jnp.bfloat16)
            sums[0, :, lanes] = dot(grad_score, query_s[:, lanes], ((1,), (0,))).astype(sums.dtype)
            back += dot(part[0, :, lanes], grad_score, ((0,), (0,)))
        low, high = back[:HALF], back[HALF:]
        back = jnp.concatenate(
            [
                low * half_cosine[...] + high * half_sine[...],
                high * half_cosine[...] - low * half_sine[...],
            ],
            axis=0,
        )
        back_s[:, lanes] = back.T.astype(jnp.bfloat16)

    scores = stage_scores(0)
    for h in range(heads):
        grad_chances = stage_grad(h)
        chances = stage_soft(scores)
        if h + 1 < heads:
            scores = stage_scores(h + 1)
        stage_out(h, chances)
        stage_back(h, chances, grad_chances)
    for result, index in results:
        place = start_of(index, result.shape[1])
        result[0] = out_s[place, :]
        result[1] = back_s[place, :]


def attend(meta, listed, half_cosine, half_sine, mid, near, far, inputs, heads):
    n = len(inputs)
    _, length, width = mid.shape
    rows, lanes = length // n, heads * HEAD_SIZE
    results = pl.pallas_call(
        functools.partial(attend_kernel, n, heads),
        out_shape=[jax.ShapeDtypeStruct((2, rows, width), jnp.bfloat16)] * n
        + [jax.ShapeDtypeStruct(mid.shape, jnp.float32)]
        + [jax.ShapeDtypeStruct(mid.shape, jnp.bfloat16)] * 2,
        in_specs=[SMEM_SPEC] * 2 + [VMEM_SPEC] * (5 + n),
        out_specs=[VMEM_SPEC] * (n + 3),
        scratch_shapes=[pltpu.VMEM((length, lanes), jnp.bfloat16)] * 4,
        compiler_params=params(),
        cost_estimate=cost(36 * length * length * width, 40 * length * width),
        name="attend",
    )(meta, listed, half_cosine, half_sine, mid, near, far, *inputs)
    return results[:n], *results[n:]


def combine_kernel(meta, cosine, sine, own, from_near, from_far, *pieces):
    for piece, index in views(meta, pieces):
        place = start_of(index, piece.shape[1])
        for h in range(0, own.shape[2], HEAD_SIZE):
            lanes = slice(h, h + HEAD_SIZE)
            for t in range(2):
                total = (
                    own[t, place, lanes]
                    + from_near[t, place, lanes].astype(jnp.float32)
                    + from_far[t, place, lanes].astype(jnp.float32)
                )
                if t == 0:
                    total = unrotate(total, cosine[place, :], sine[place, :])
                piece[t, :, lanes] = total.astype(jnp.bfloat16)


def combine(meta, cosine, sine, own, from_near, from_far, n):
    _, length, width = own.shape
    return pl.pallas_call(
        combine_kernel,
        out_shape=[jax.ShapeDtypeStruct((2, length // n, width), jnp.bfloat16)] * n,
        in_specs=[SMEM_SPEC] + [VMEM_SPEC] * 5,
        out_specs=[VMEM_SPEC] * n,
        compiler_params=params(),
        cost_estimate=cost(0, 20 * length * width),
        name="combine",
    )(meta, cosine, sine, own, from_far, from_near)


def join_kernel(n, meta, *refs):
    pieces, outs, sems = refs[:n], refs[n:-1], refs[-1]
    copies = []
    for step, piece in enumerate(pieces):
        lanes = start_of(jnp.bitwise_xor(meta[0], step), piece.shape[2])
        for t, out in enumerate(outs):
            copies.append(pltpu.make_async_copy(piece.at[t], out.at[:, lanes], sems.at[step, t]))
    for copy in copies:
        copy.start()
    for copy in copies:
        copy.wait()


def join(meta, pieces):
    n = len(pieces)
    count, rows, width = pieces[0].shape
    return pl.pallas_call(
        functools.partial(join_kernel, n),
        out_shape=[jax.ShapeDtypeStruct((rows, n * width), jnp.bfloat16)] * count,
        in_specs=[SMEM_SPEC] + [ANY_SPEC] * n,
        out_specs=[HBM_SPEC] * count,
        scratch_shapes=[pltpu.SemaphoreType.DMA((n, count))],
        compiler_params=params(),
        cost_estimate=cost(0, 4 * n * count * rows * width),
        name="join",
    )(meta, *pieces)


def swap(pieces):
    if len(pieces) == 1:
        return [lax.all_to_all(pieces[0], "head", 0, 0, tiled=True)]
    n = len(pieces)
    return [pieces[0]] + [
        lax.ppermute(pieces[k], "head", [(i, i ^ k) for i in range(n)]) for k in range(1, n)
    ]


def trade(block, first):
    route = []
    for i in range(first, lax.axis_size("seq") - 1, 2):
        route += [(i, i + 1), (i + 1, i)]
    return lax.ppermute(block, "seq", route)


def on_device(queries, keys, values, out_grad, chain_lengths, block_pairs):
    n = lax.axis_size("head")
    length = queries.shape[0] * n
    meta = jnp.stack([lax.axis_index("head"), lax.axis_index("seq")]).astype(jnp.int32)
    key_value = swap(cut(meta, chain_lengths, keys, values, n, WIDE_LIMIT))
    later = cut(meta, chain_lengths, queries, out_grad, n, VMEM_LIMIT, [key_value[1]])
    inputs = swap(later)
    mid = order(meta, key_value, [later[0]])
    far, near = trade(mid, 1), trade(again(mid, [inputs[1]]), 0)
    cosine, sine, half_cosine, half_sine = tables(meta, chain_lengths, length, [inputs[1]])
    results, own, near_sum, far_sum = attend(
        meta, block_pairs, half_cosine, half_sine, mid, near, far, inputs, HEADS_A_STEP
    )
    back_out = swap(results)
    attn_out, query_grad = join(meta, back_out)
    from_far, from_near = trade(far_sum, 1), trade(near_sum, 0)
    back = swap(combine(meta, cosine, sine, own, from_near, from_far, n))
    key_grad, value_grad = join(meta, back)
    return attn_out, query_grad, key_grad, value_grad


def solution(mesh):
    split = P(("seq", "head"), None)
    return jax.shard_map(
        on_device,
        mesh=mesh,
        in_specs=(split, split, split, split, P(), P()),
        out_specs=(split, split, split, split),
        check_vma=False,
    )
```

```python
import functools
import math

import jax
import jax.numpy as jnp
from jax import lax
from jax.experimental import pallas as pl
from jax.experimental.pallas import tpu as pltpu
from jax.sharding import PartitionSpec as P

HEAD_SIZE = 128
BLOCK_TOKENS = 128
HALF = HEAD_SIZE // 2
SCALE = 1.0 / math.sqrt(HEAD_SIZE)
VMEM_LIMIT = 32 * 1024 * 1024
WIDE_LIMIT = 60 * 1024 * 1024
HEADS_A_STEP = 10

masked_score = -1e30
rotary_base = 10000.0

SMEM_SPEC = pl.BlockSpec(memory_space=pltpu.SMEM)


def cost(flops, moved, exps=0):
    return pl.CostEstimate(flops=flops, bytes_accessed=moved, transcendentals=exps)


def params(limit=VMEM_LIMIT):
    return pltpu.CompilerParams(vmem_limit_bytes=limit)


def behind(kernel, count):
    def run(*refs):
        kernel(*refs[count:])

    return run if count else kernel


ANY_SPEC = pl.BlockSpec(memory_space=pl.ANY)
HBM_SPEC = pl.BlockSpec(memory_space=pltpu.HBM)
VMEM_SPEC = pl.BlockSpec(memory_space=pltpu.VMEM)


def chain_angles(lengths, first_row, shape, tokens):
    row = first_row + lax.broadcasted_iota(jnp.int32, shape, tokens)

    def look(c, carry):
        start, begin = carry
        return start + lengths[c], jnp.maximum(begin, jnp.where(row >= start, start, 0))

    _, begin = lax.fori_loop(
        0, lengths.shape[0], look, (jnp.int32(0), jnp.zeros(shape, jnp.int32))
    )
    entry = lax.broadcasted_iota(jnp.int32, shape, 1 - tokens)
    column = jnp.where(entry < HALF, entry, entry - HALF).astype(jnp.float32)
    frequency = jnp.exp(column * (-2.0 * math.log(rotary_base) / HEAD_SIZE))
    return (row - begin).astype(jnp.float32) * frequency, entry


def fill_tables(lengths, first_row, cosine, sine):
    angle, entry = chain_angles(lengths, first_row, cosine.shape, 0)
    turn = jnp.sin(angle)
    cosine[...] = jnp.cos(angle)
    sine[...] = jnp.where(entry < HALF, -turn, turn)


def rotate(x, cosine, sine):
    return x * cosine + pltpu.roll(x, HALF, 1) * sine


def unrotate(g, cosine, sine):
    return g * cosine - pltpu.roll(g, HALF, 1) * sine


def views(meta, refs):
    if len(refs) == 1:
        return [(refs[0].at[i], i) for i in range(refs[0].shape[0])]
    return [(ref, jnp.bitwise_xor(meta[0], k)) for k, ref in enumerate(refs)]


def start_of(index, size):
    return pl.ds(index * size if isinstance(index, int) else pl.multiple_of(index * size, size), size)


def set_shapes(joined, n, shape, dtype=jnp.bfloat16):
    if joined:
        return [jax.ShapeDtypeStruct((n,) + shape, dtype)]
    return [jax.ShapeDtypeStruct(shape, dtype)] * n


def set_specs(joined, n, shape, index_map):
    if joined:
        return [pl.BlockSpec((n,) + shape, lambda *i: (0,) + index_map(*i))]
    return [pl.BlockSpec(shape, index_map)] * n


def again_kernel(value, out):
    out[...] = value[...]


def again(value, after):
    return pl.pallas_call(
        behind(again_kernel, len(after)),
        out_shape=jax.ShapeDtypeStruct(value.shape, value.dtype),
        in_specs=[ANY_SPEC] * len(after) + [VMEM_SPEC],
        out_specs=VMEM_SPEC,
        compiler_params=params(),
        cost_estimate=cost(0, 2 * value.size),
        name="again",
    )(*after, value)


def dot(a, b, contract):
    return lax.dot_general(a, b, (contract, ((), ())), preferred_element_type=jnp.float32)


def cut_kernel(n, lengths, turned, plain, *refs):
    meta = lax.axis_index("head"), lax.axis_index("seq")
    pieces, (held, cosine, sine, sems) = refs[-4 - n : -4], refs[-4:]
    rows, width = turned.shape[0], held.shape[2]
    copies = []
    for step, piece in enumerate(pieces):
        lanes = start_of(jnp.bitwise_xor(meta[0], step), width)
        copies.append(
            (
                pltpu.make_async_copy(turned.at[:, lanes], held.at[step], sems.at[step, 0]),
                pltpu.make_async_copy(plain.at[:, lanes], piece.at[1], sems.at[step, 1]),
            )
        )
    for t in range(2):
        for step in range(n):
            copies[step][t].start()
    fill_tables(lengths, meta[1] * (rows * n) + meta[0] * rows, cosine, sine)
    for step, piece in enumerate(pieces):
        copies[step][0].wait()
        for h in range(0, width, HEAD_SIZE):
            lanes = slice(h, h + HEAD_SIZE)
            x = held[step, :, lanes].astype(jnp.float32)
            piece[0, :, lanes] = rotate(x, cosine[...], sine[...]).astype(jnp.bfloat16)
    for step in range(n):
        copies[step][1].wait()


def cut(lengths, turned, plain, n, limit, after=()):
    rows, width = turned.shape[0], turned.shape[1] // n
    return pl.pallas_call(
        functools.partial(cut_kernel, n),
        out_shape=[jax.ShapeDtypeStruct((2, rows, width), jnp.bfloat16)] * n,
        in_specs=[SMEM_SPEC] + [HBM_SPEC] * 2 + [ANY_SPEC] * len(after),
        out_specs=[VMEM_SPEC] * n,
        scratch_shapes=[
            pltpu.VMEM((n, rows, width), jnp.bfloat16),
            pltpu.VMEM((rows, HEAD_SIZE), jnp.float32),
            pltpu.VMEM((rows, HEAD_SIZE), jnp.float32),
            pltpu.SemaphoreType.DMA((n, 2)),
        ],
        compiler_params=params(limit),
        cost_estimate=cost(0, 8 * n * rows * width),
        name="cut",
    )(lengths, turned, plain, *after)


def tables_kernel(meta, lengths, cosine, sine, half_cosine, half_sine):
    first = meta[1] * cosine.shape[0]
    fill_tables(lengths, first, cosine, sine)
    angle, _ = chain_angles(lengths, first, half_cosine.shape, 1)
    half_cosine[...] = jnp.cos(angle)
    half_sine[...] = jnp.sin(angle)


def tables(meta, lengths, length, after):
    return pl.pallas_call(
        behind(tables_kernel, len(after)),
        out_shape=[jax.ShapeDtypeStruct((length, HEAD_SIZE), jnp.float32)] * 2
        + [jax.ShapeDtypeStruct((HALF, length), jnp.float32)] * 2,
        in_specs=[ANY_SPEC] * len(after) + [SMEM_SPEC] * 2,
        compiler_params=params(),
        cost_estimate=cost(0, 8 * length * HEAD_SIZE),
        name="tables",
    )(*after, meta, lengths)


def order_kernel(meta, *refs):
    out = refs[-1]
    for piece, index in views(meta, refs[:-1]):
        out[:, start_of(index, piece.shape[1]), :] = piece[...]


def order(meta, pieces, after=()):
    _, rows, width = pieces[0].shape
    n = len(pieces)
    return pl.pallas_call(
        behind(order_kernel, len(after)),
        out_shape=jax.ShapeDtypeStruct((2, n * rows, width), jnp.bfloat16),
        in_specs=[ANY_SPEC] * len(after) + [SMEM_SPEC] + [VMEM_SPEC] * n,
        out_specs=VMEM_SPEC,
        compiler_params=params(),
        cost_estimate=cost(0, 8 * n * rows * width),
        name="order",
    )(*after, meta, *pieces)


def window_shards(shard):
    odd = lax.rem(shard, 2)
    return shard, shard + 1 - 2 * odd, shard - 1 + 2 * odd


def attend_kernel(count, heads, meta, listed, half_cosine, half_sine, mid, near, far, *refs):
    inputs, results = views(meta, refs[:count]), views(meta, refs[count:-7])
    own, near_sum, far_sum, query_s, grad_s, out_s, back_s = refs[-7:]
    length = mid.shape[1]
    nblk = length // BLOCK_TOKENS
    for piece, index in inputs:
        place = start_of(index, piece.shape[1])
        query_s[place, :] = piece[0]
        grad_s[place, :] = piece[1]
    first = meta[1] * nblk
    query_block = lax.broadcasted_iota(jnp.int32, (1, length), 1) // BLOCK_TOKENS
    addends = []
    for shard in window_shards(meta[1]):
        for key_block in range(nblk):
            addend = jnp.zeros((1, length), jnp.float32)
            for block in range(nblk):
                times = jnp.int32(0)
                for p in range(listed.shape[1]):
                    entry = listed[first + block, p]
                    times += jnp.where((entry >= 0) & (entry == shard * nblk + key_block), 1, 0)
                addend = jnp.where(query_block == block, times.astype(jnp.float32), addend)
            addends.append(jnp.where(addend > 0, jnp.log2(jnp.maximum(addend, 1.0)), masked_score))
    window = ((mid, own), (near, near_sum), (far, far_sum))
    def lanes_of(h):
        return slice(h * HEAD_SIZE, (h + 1) * HEAD_SIZE)

    def stage_scores(h):
        lanes, scores = lanes_of(h), []
        for i, (part, _) in enumerate(window):
            score = dot(part[0, :, lanes], query_s[:, lanes], ((1,), (1,))) * (SCALE * math.log2(math.e))
            for b in range(nblk):
                block = score[b * BLOCK_TOKENS : (b + 1) * BLOCK_TOKENS]
                scores.append(block + addends[i * nblk + b])
        return scores

    def stage_grad(h):
        lanes = lanes_of(h)
        return [dot(part[1, :, lanes], grad_s[:, lanes], ((1,), (1,))) for part, _ in window]

    def stage_soft(scores):
        top = functools.reduce(jnp.maximum, [jnp.max(s, axis=0, keepdims=True) for s in scores])
        raised = [jnp.exp2(s - top) for s in scores]
        scaling = 1.0 / sum(jnp.sum(r, axis=0, keepdims=True) for r in raised)
        return [jnp.concatenate(raised[i * nblk : (i + 1) * nblk], axis=0) * scaling for i in range(3)]

    def stage_out(h, chances):
        lanes = lanes_of(h)
        out = jnp.zeros((HEAD_SIZE, length), jnp.float32)
        for (part, sums), chance in zip(window, chances):
            weights = chance.astype(jnp.bfloat16)
            sums[1, :, lanes] = dot(weights, grad_s[:, lanes], ((1,), (0,))).astype(sums.dtype)
            out += dot(part[1, :, lanes], weights, ((0,), (0,)))
        out_s[:, lanes] = out.astype(jnp.bfloat16).T

    def stage_back(h, chances, grad_chances):
        lanes = lanes_of(h)
        delta = sum(jnp.sum(c * g, axis=0, keepdims=True) for c, g in zip(chances, grad_chances))
        back = jnp.zeros((HEAD_SIZE, length), jnp.float32)
        for (part, sums), c, g in zip(window, chances, grad_chances):
            grad_score = (c * (g - delta) * SCALE).astype(jnp.bfloat16)
            sums[0, :, lanes] = dot(grad_score, query_s[:, lanes], ((1,), (0,))).astype(sums.dtype)
            back += dot(part[0, :, lanes], grad_score, ((0,), (0,)))
        low, high = back[:HALF], back[HALF:]
        back = jnp.concatenate(
            [
                low * half_cosine[...] + high * half_sine[...],
                high * half_cosine[...] - low * half_sine[...],
            ],
            axis=0,
        )
        back_s[:, lanes] = back.astype(jnp.bfloat16).T

    scores, grad_chances = stage_scores(0), stage_grad(0)
    for h in range(heads):
        chances = stage_soft(scores)
        if h + 1 < heads:
            scores = stage_scores(h + 1)
        stage_back(h, chances, grad_chances)
        if h + 1 < heads:
            grad_chances = stage_grad(h + 1)
        stage_out(h, chances)
    for result, index in results:
        place = start_of(index, result.shape[1])
        result[0] = out_s[place, :]
        result[1] = back_s[place, :]


def attend(meta, listed, half_cosine, half_sine, mid, near, far, inputs, heads):
    n = len(inputs)
    _, length, width = mid.shape
    rows, lanes = length // n, heads * HEAD_SIZE
    results = pl.pallas_call(
        functools.partial(attend_kernel, n, heads),
        out_shape=[jax.ShapeDtypeStruct((2, rows, width), jnp.bfloat16)] * n
        + [jax.ShapeDtypeStruct(mid.shape, jnp.float32)]
        + [jax.ShapeDtypeStruct(mid.shape, jnp.bfloat16)] * 2,
        in_specs=[SMEM_SPEC] * 2 + [VMEM_SPEC] * (5 + n),
        out_specs=[VMEM_SPEC] * (n + 3),
        scratch_shapes=[pltpu.VMEM((length, lanes), jnp.bfloat16)] * 4,
        compiler_params=params(),
        cost_estimate=cost(36 * length * length * width, 40 * length * width),
        name="attend",
    )(meta, listed, half_cosine, half_sine, mid, near, far, *inputs)
    return results[:n], *results[n:]


def combine_kernel(meta, cosine, sine, own, from_near, from_far, *pieces):
    for piece, index in views(meta, pieces):
        place = start_of(index, piece.shape[1])
        for h in range(0, own.shape[2], HEAD_SIZE):
            lanes = slice(h, h + HEAD_SIZE)
            for t in range(2):
                total = (
                    own[t, place, lanes]
                    + from_near[t, place, lanes].astype(jnp.float32)
                    + from_far[t, place, lanes].astype(jnp.float32)
                )
                if t == 0:
                    total = unrotate(total, cosine[place, :], sine[place, :])
                piece[t, :, lanes] = total.astype(jnp.bfloat16)


def combine(meta, cosine, sine, own, from_near, from_far, n):
    _, length, width = own.shape
    return pl.pallas_call(
        combine_kernel,
        out_shape=[jax.ShapeDtypeStruct((2, length // n, width), jnp.bfloat16)] * n,
        in_specs=[SMEM_SPEC] + [VMEM_SPEC] * 5,
        out_specs=[VMEM_SPEC] * n,
        compiler_params=params(),
        cost_estimate=cost(0, 20 * length * width),
        name="combine",
    )(meta, cosine, sine, own, from_far, from_near)


def join_kernel(n, meta, *refs):
    pieces, outs, sems = refs[:n], refs[n:-1], refs[-1]
    copies = []
    for step, piece in enumerate(pieces):
        lanes = start_of(jnp.bitwise_xor(meta[0], step), piece.shape[2])
        for t, out in enumerate(outs):
            copies.append(pltpu.make_async_copy(piece.at[t], out.at[:, lanes], sems.at[step, t]))
    for copy in copies:
        copy.start()
    for copy in copies:
        copy.wait()


def join(meta, pieces):
    n = len(pieces)
    count, rows, width = pieces[0].shape
    return pl.pallas_call(
        functools.partial(join_kernel, n),
        out_shape=[jax.ShapeDtypeStruct((rows, n * width), jnp.bfloat16)] * count,
        in_specs=[SMEM_SPEC] + [ANY_SPEC] * n,
        out_specs=[HBM_SPEC] * count,
        scratch_shapes=[pltpu.SemaphoreType.DMA((n, count))],
        compiler_params=params(),
        cost_estimate=cost(0, 4 * n * count * rows * width),
        name="join",
    )(meta, *pieces)


def swap(pieces):
    if len(pieces) == 1:
        return [lax.all_to_all(pieces[0], "head", 0, 0, tiled=True)]
    n = len(pieces)
    return [pieces[0]] + [
        lax.ppermute(pieces[k], "head", [(i, i ^ k) for i in range(n)]) for k in range(1, n)
    ]


def trade(block, first):
    route = []
    for i in range(first, lax.axis_size("seq") - 1, 2):
        route += [(i, i + 1), (i + 1, i)]
    return lax.ppermute(block, "seq", route)


def on_device(queries, keys, values, out_grad, chain_lengths, block_pairs):
    n = lax.axis_size("head")
    length = queries.shape[0] * n
    meta = jnp.stack([lax.axis_index("head"), lax.axis_index("seq")]).astype(jnp.int32)
    key_value = swap(cut(chain_lengths, keys, values, n, WIDE_LIMIT))
    later = cut(chain_lengths, queries, out_grad, n, VMEM_LIMIT, [key_value[1]])
    inputs = swap(later)
    mid = order(meta, key_value, [later[0]])
    far, near = trade(mid, 1), trade(again(mid, [inputs[1]]), 0)
    cosine, sine, half_cosine, half_sine = tables(meta, chain_lengths, length, [inputs[1]])
    results, own, near_sum, far_sum = attend(
        meta, block_pairs, half_cosine, half_sine, mid, near, far, inputs, HEADS_A_STEP
    )
    back_out = swap(results)
    attn_out, query_grad = join(meta, back_out)
    from_far, from_near = trade(far_sum, 1), trade(near_sum, 0)
    back = swap(combine(meta, cosine, sine, own, from_near, from_far, n))
    key_grad, value_grad = join(meta, back)
    return attn_out, query_grad, key_grad, value_grad


def solution(mesh):
    split = P(("seq", "head"), None)
    return jax.shard_map(
        on_device,
        mesh=mesh,
        in_specs=(split, split, split, split, P(), P()),
        out_specs=(split, split, split, split),
        check_vma=False,
    )
```

```python
import functools
import math

import jax
import jax.numpy as jnp
from jax import lax
from jax.experimental import pallas as pl
from jax.experimental.pallas import tpu as pltpu
from jax.sharding import PartitionSpec as P

HEAD_SIZE = 128
BLOCK_TOKENS = 128
HALF = HEAD_SIZE // 2
SCALE = 1.0 / math.sqrt(HEAD_SIZE)
VMEM_LIMIT = 32 * 1024 * 1024
WIDE_LIMIT = 60 * 1024 * 1024
HEADS_A_STEP = 10

masked_score = -1e30
rotary_base = 10000.0

SMEM_SPEC = pl.BlockSpec(memory_space=pltpu.SMEM)


def cost(flops, moved, exps=0):
    return pl.CostEstimate(flops=flops, bytes_accessed=moved, transcendentals=exps)


def params(limit=VMEM_LIMIT):
    return pltpu.CompilerParams(vmem_limit_bytes=limit)


def behind(kernel, count):
    def run(*refs):
        kernel(*refs[count:])

    return run if count else kernel


ANY_SPEC = pl.BlockSpec(memory_space=pl.ANY)
HBM_SPEC = pl.BlockSpec(memory_space=pltpu.HBM)
VMEM_SPEC = pl.BlockSpec(memory_space=pltpu.VMEM)


def chain_angles(lengths, first_row, shape, tokens):
    row = first_row + lax.broadcasted_iota(jnp.int32, shape, tokens)

    def look(c, carry):
        start, begin = carry
        return start + lengths[c], jnp.maximum(begin, jnp.where(row >= start, start, 0))

    _, begin = lax.fori_loop(
        0, lengths.shape[0], look, (jnp.int32(0), jnp.zeros(shape, jnp.int32))
    )
    entry = lax.broadcasted_iota(jnp.int32, shape, 1 - tokens)
    column = jnp.where(entry < HALF, entry, entry - HALF).astype(jnp.float32)
    frequency = jnp.exp(column * (-2.0 * math.log(rotary_base) / HEAD_SIZE))
    return (row - begin).astype(jnp.float32) * frequency, entry


def fill_tables(lengths, first_row, cosine, sine):
    angle, entry = chain_angles(lengths, first_row, cosine.shape, 0)
    turn = jnp.sin(angle)
    cosine[...] = jnp.cos(angle)
    sine[...] = jnp.where(entry < HALF, -turn, turn)


def rotate(x, cosine, sine):
    return x * cosine + pltpu.roll(x, HALF, 1) * sine


def unrotate(g, cosine, sine):
    return g * cosine - pltpu.roll(g, HALF, 1) * sine


def views(meta, refs):
    if len(refs) == 1:
        return [(refs[0].at[i], i) for i in range(refs[0].shape[0])]
    return [(ref, jnp.bitwise_xor(meta[0], k)) for k, ref in enumerate(refs)]


def start_of(index, size):
    return pl.ds(index * size if isinstance(index, int) else pl.multiple_of(index * size, size), size)


def set_shapes(joined, n, shape, dtype=jnp.bfloat16):
    if joined:
        return [jax.ShapeDtypeStruct((n,) + shape, dtype)]
    return [jax.ShapeDtypeStruct(shape, dtype)] * n


def set_specs(joined, n, shape, index_map):
    if joined:
        return [pl.BlockSpec((n,) + shape, lambda *i: (0,) + index_map(*i))]
    return [pl.BlockSpec(shape, index_map)] * n


def again_kernel(value, out):
    out[...] = value[...]


def again(value, after):
    return pl.pallas_call(
        behind(again_kernel, len(after)),
        out_shape=jax.ShapeDtypeStruct(value.shape, value.dtype),
        in_specs=[ANY_SPEC] * len(after) + [VMEM_SPEC],
        out_specs=VMEM_SPEC,
        compiler_params=params(),
        cost_estimate=cost(0, 2 * value.size),
        name="again",
    )(*after, value)


def dot(a, b, contract):
    return lax.dot_general(a, b, (contract, ((), ())), preferred_element_type=jnp.float32)


def cut_kernel(n, lengths, turned, plain, *refs):
    meta = lax.axis_index("head"), lax.axis_index("seq")
    pieces, (held, cosine, sine, sems) = refs[-4 - n : -4], refs[-4:]
    rows, width = turned.shape[0], held.shape[2]
    copies = []
    for step, piece in enumerate(pieces):
        lanes = start_of(jnp.bitwise_xor(meta[0], step), width)
        copies.append(
            (
                pltpu.make_async_copy(turned.at[:, lanes], held.at[step], sems.at[step, 0]),
                pltpu.make_async_copy(plain.at[:, lanes], piece.at[1], sems.at[step, 1]),
            )
        )
    for t in range(2):
        for step in range(n):
            copies[step][t].start()
    fill_tables(lengths, meta[1] * (rows * n) + meta[0] * rows, cosine, sine)
    for step, piece in enumerate(pieces):
        copies[step][0].wait()
        for h in range(0, width, HEAD_SIZE):
            lanes = slice(h, h + HEAD_SIZE)
            x = held[step, :, lanes].astype(jnp.float32)
            piece[0, :, lanes] = rotate(x, cosine[...], sine[...]).astype(jnp.bfloat16)
    for step in range(n):
        copies[step][1].wait()


def cut(lengths, turned, plain, n, limit, after=()):
    rows, width = turned.shape[0], turned.shape[1] // n
    return pl.pallas_call(
        functools.partial(cut_kernel, n),
        out_shape=[jax.ShapeDtypeStruct((2, rows, width), jnp.bfloat16)] * n,
        in_specs=[SMEM_SPEC] + [HBM_SPEC] * 2 + [ANY_SPEC] * len(after),
        out_specs=[VMEM_SPEC] * n,
        scratch_shapes=[
            pltpu.VMEM((n, rows, width), jnp.bfloat16),
            pltpu.VMEM((rows, HEAD_SIZE), jnp.float32),
            pltpu.VMEM((rows, HEAD_SIZE), jnp.float32),
            pltpu.SemaphoreType.DMA((n, 2)),
        ],
        compiler_params=params(limit),
        cost_estimate=cost(0, 8 * n * rows * width),
        name="cut",
    )(lengths, turned, plain, *after)


def tables_kernel(meta, lengths, cosine, sine, half_cosine, half_sine):
    first = meta[1] * cosine.shape[0]
    fill_tables(lengths, first, cosine, sine)
    angle, _ = chain_angles(lengths, first, half_cosine.shape, 1)
    half_cosine[...] = jnp.cos(angle)
    half_sine[...] = jnp.sin(angle)


def tables(meta, lengths, length, after):
    return pl.pallas_call(
        behind(tables_kernel, len(after)),
        out_shape=[jax.ShapeDtypeStruct((length, HEAD_SIZE), jnp.float32)] * 2
        + [jax.ShapeDtypeStruct((HALF, length), jnp.float32)] * 2,
        in_specs=[ANY_SPEC] * len(after) + [SMEM_SPEC] * 2,
        compiler_params=params(),
        cost_estimate=cost(0, 8 * length * HEAD_SIZE),
        name="tables",
    )(*after, meta, lengths)


def order_kernel(meta, *refs):
    out = refs[-1]
    for piece, index in views(meta, refs[:-1]):
        out[:, start_of(index, piece.shape[1]), :] = piece[...]


def order(meta, pieces, after=()):
    _, rows, width = pieces[0].shape
    n = len(pieces)
    return pl.pallas_call(
        behind(order_kernel, len(after)),
        out_shape=jax.ShapeDtypeStruct((2, n * rows, width), jnp.bfloat16),
        in_specs=[ANY_SPEC] * len(after) + [SMEM_SPEC] + [VMEM_SPEC] * n,
        out_specs=VMEM_SPEC,
        compiler_params=params(),
        cost_estimate=cost(0, 8 * n * rows * width),
        name="order",
    )(*after, meta, *pieces)


def window_shards(shard):
    odd = lax.rem(shard, 2)
    return shard, shard + 1 - 2 * odd, shard - 1 + 2 * odd


def attend_kernel(count, heads, meta, listed, half_cosine, half_sine, mid, near, far, *refs):
    inputs, results = views(meta, refs[:count]), views(meta, refs[count:-7])
    own, near_sum, far_sum, query_s, grad_s, out_s, back_s = refs[-7:]
    length = mid.shape[1]
    nblk = length // BLOCK_TOKENS
    for piece, index in inputs:
        place = start_of(index, piece.shape[1])
        query_s[place, :] = piece[0]
        grad_s[place, :] = piece[1]
    first = meta[1] * nblk
    query_block = lax.broadcasted_iota(jnp.int32, (1, length), 1) // BLOCK_TOKENS
    addends = []
    for shard in window_shards(meta[1]):
        for key_block in range(nblk):
            addend = jnp.zeros((1, length), jnp.float32)
            for block in range(nblk):
                times = jnp.int32(0)
                for p in range(listed.shape[1]):
                    entry = listed[first + block, p]
                    times += jnp.where((entry >= 0) & (entry == shard * nblk + key_block), 1, 0)
                addend = jnp.where(query_block == block, times.astype(jnp.float32), addend)
            addends.append(jnp.where(addend > 0, jnp.log2(jnp.maximum(addend, 1.0)), masked_score))
    window = ((mid, own), (near, near_sum), (far, far_sum))
    def lanes_of(h):
        return slice(h * HEAD_SIZE, (h + 1) * HEAD_SIZE)

    def stage_scores(h):
        lanes, scores = lanes_of(h), []
        for i, (part, _) in enumerate(window):
            score = dot(part[0, :, lanes], query_s[:, lanes], ((1,), (1,))) * (SCALE * math.log2(math.e))
            for b in range(nblk):
                block = score[b * BLOCK_TOKENS : (b + 1) * BLOCK_TOKENS]
                scores.append(block + addends[i * nblk + b])
        return scores

    def stage_grad(h):
        lanes = lanes_of(h)
        return [dot(part[1, :, lanes], grad_s[:, lanes], ((1,), (1,))) for part, _ in window]

    def stage_soft(scores):
        top = functools.reduce(jnp.maximum, [jnp.max(s, axis=0, keepdims=True) for s in scores])
        raised = [jnp.exp2(s - top) for s in scores]
        scaling = 1.0 / sum(jnp.sum(r, axis=0, keepdims=True) for r in raised)
        return [jnp.concatenate(raised[i * nblk : (i + 1) * nblk], axis=0) * scaling for i in range(3)]

    def stage_out(h, chances):
        lanes = lanes_of(h)
        out = jnp.zeros((HEAD_SIZE, length), jnp.float32)
        for (part, sums), chance in zip(window, chances):
            weights = chance.astype(jnp.bfloat16)
            sums[1, :, lanes] = dot(weights, grad_s[:, lanes], ((1,), (0,))).astype(sums.dtype)
            out += dot(part[1, :, lanes], weights, ((0,), (0,)))
        out_s[:, lanes] = out.astype(jnp.bfloat16).T

    def stage_back(h, chances, grad_chances):
        lanes = lanes_of(h)
        delta = sum(jnp.sum(c * g, axis=0, keepdims=True) for c, g in zip(chances, grad_chances))
        back = jnp.zeros((HEAD_SIZE, length), jnp.float32)
        for (part, sums), c, g in zip(window, chances, grad_chances):
            grad_score = (c * (g - delta) * SCALE).astype(jnp.bfloat16)
            sums[0, :, lanes] = dot(grad_score, query_s[:, lanes], ((1,), (0,))).astype(sums.dtype)
            back += dot(part[0, :, lanes], grad_score, ((0,), (0,)))
        low, high = back[:HALF], back[HALF:]
        back = jnp.concatenate(
            [
                low * half_cosine[...] + high * half_sine[...],
                high * half_cosine[...] - low * half_sine[...],
            ],
            axis=0,
        )
        back_s[:, lanes] = back.astype(jnp.bfloat16).T

    scores, grad_chances = stage_scores(0), stage_grad(0)
    for h in range(heads):
        chances = stage_soft(scores)
        if h + 1 < heads:
            scores = stage_scores(h + 1)
        stage_back(h, chances, grad_chances)
        if h + 1 < heads:
            grad_chances = stage_grad(h + 1)
        stage_out(h, chances)
    for result, index in results:
        place = start_of(index, result.shape[1])
        result[0] = out_s[place, :]
        result[1] = back_s[place, :]


def attend(meta, listed, half_cosine, half_sine, mid, near, far, inputs, heads):
    n = len(inputs)
    _, length, width = mid.shape
    rows, lanes = length // n, heads * HEAD_SIZE
    results = pl.pallas_call(
        functools.partial(attend_kernel, n, heads),
        out_shape=[jax.ShapeDtypeStruct((2, rows, width), jnp.bfloat16)] * n
        + [jax.ShapeDtypeStruct(mid.shape, jnp.float32)]
        + [jax.ShapeDtypeStruct(mid.shape, jnp.bfloat16)] * 2,
        in_specs=[SMEM_SPEC] * 2 + [VMEM_SPEC] * (5 + n),
        out_specs=[VMEM_SPEC] * (n + 3),
        scratch_shapes=[pltpu.VMEM((length, lanes), jnp.bfloat16)] * 4,
        compiler_params=params(),
        cost_estimate=cost(36 * length * length * width, 40 * length * width),
        name="attend",
    )(meta, listed, half_cosine, half_sine, mid, near, far, *inputs)
    return results[:n], *results[n:]


def combine_kernel(meta, cosine, sine, own, from_near, from_far, *pieces):
    for piece, index in views(meta, pieces):
        place = start_of(index, piece.shape[1])
        for h in range(0, own.shape[2], HEAD_SIZE):
            lanes = slice(h, h + HEAD_SIZE)
            for t in range(2):
                total = (
                    own[t, place, lanes]
                    + from_near[t, place, lanes].astype(jnp.float32)
                    + from_far[t, place, lanes].astype(jnp.float32)
                )
                if t == 0:
                    total = unrotate(total, cosine[place, :], sine[place, :])
                piece[t, :, lanes] = total.astype(jnp.bfloat16)


def combine(meta, cosine, sine, own, from_near, from_far, n):
    _, length, width = own.shape
    return pl.pallas_call(
        combine_kernel,
        out_shape=[jax.ShapeDtypeStruct((2, length // n, width), jnp.bfloat16)] * n,
        in_specs=[SMEM_SPEC] + [VMEM_SPEC] * 5,
        out_specs=[VMEM_SPEC] * n,
        compiler_params=params(),
        cost_estimate=cost(0, 20 * length * width),
        name="combine",
    )(meta, cosine, sine, own, from_far, from_near)


def join_kernel(steps, meta, *refs):
    pieces, outs, sems = refs[: len(steps)], refs[-3:-1], refs[-1]
    copies = []
    for i, (step, piece) in enumerate(zip(steps, pieces)):
        lanes = start_of(jnp.bitwise_xor(meta[0], step), piece.shape[2])
        for t, out in enumerate(outs):
            copies.append(pltpu.make_async_copy(piece.at[t], out.at[:, lanes], sems.at[i, t]))
    for copy in copies:
        copy.start()
    for copy in copies:
        copy.wait()


def join(meta, pieces, steps, outs=()):
    n = len(pieces)
    count, rows, width = pieces[0].shape
    chosen = [pieces[step] for step in steps]
    return pl.pallas_call(
        functools.partial(join_kernel, steps),
        out_shape=[jax.ShapeDtypeStruct((rows, n * width), jnp.bfloat16)] * count,
        in_specs=[SMEM_SPEC] + [ANY_SPEC] * len(steps) + [HBM_SPEC] * len(outs),
        out_specs=[HBM_SPEC] * count,
        scratch_shapes=[pltpu.SemaphoreType.DMA((len(steps), count))],
        input_output_aliases={1 + len(steps) + t: t for t in range(len(outs))},
        compiler_params=params(),
        cost_estimate=cost(0, 4 * len(steps) * count * rows * width),
        name="join",
    )(meta, *chosen, *outs)


def swap(pieces):
    if len(pieces) == 1:
        return [lax.all_to_all(pieces[0], "head", 0, 0, tiled=True)]
    n = len(pieces)
    return [pieces[0]] + [
        lax.ppermute(pieces[k], "head", [(i, i ^ k) for i in range(n)]) for k in range(1, n)
    ]


def trade(block, first):
    route = []
    for i in range(first, lax.axis_size("seq") - 1, 2):
        route += [(i, i + 1), (i + 1, i)]
    return lax.ppermute(block, "seq", route)


def on_device(queries, keys, values, out_grad, chain_lengths, block_pairs):
    n = lax.axis_size("head")
    length = queries.shape[0] * n
    meta = jnp.stack([lax.axis_index("head"), lax.axis_index("seq")]).astype(jnp.int32)
    key_value = swap(cut(chain_lengths, keys, values, n, WIDE_LIMIT))
    later = cut(chain_lengths, queries, out_grad, n, VMEM_LIMIT, [key_value[1]])
    inputs = swap(later)
    mid = order(meta, key_value, [later[0]])
    far, near = trade(mid, 1), trade(again(mid, [inputs[1]]), 0)
    cosine, sine, half_cosine, half_sine = tables(meta, chain_lengths, length, [inputs[1]])
    results, own, near_sum, far_sum = attend(
        meta, block_pairs, half_cosine, half_sine, mid, near, far, inputs, HEADS_A_STEP
    )
    back_out = swap(results)
    attn_out, query_grad = join(meta, back_out, tuple(range(n)))
    from_far, from_near = trade(far_sum, 1), trade(near_sum, 0)
    back = swap(combine(meta, cosine, sine, own, from_near, from_far, n))
    key_grad, value_grad = join(meta, back, (0, 1))
    key_grad, value_grad = join(meta, back, tuple(range(2, n)), (key_grad, value_grad))
    return attn_out, query_grad, key_grad, value_grad


def solution(mesh):
    split = P(("seq", "head"), None)
    return jax.shard_map(
        on_device,
        mesh=mesh,
        in_specs=(split, split, split, split, P(), P()),
        out_specs=(split, split, split, split),
        check_vma=False,
    )
```
